256 devices in a mesh: wide: 32 (over z, y), narrow: 8 (over x, core).
Axes of the slice: x: 4, y: 4, z: 8, core: 2. Of those that a mesh axis runs over, the one named last changes fastest.
Arguments:
- values: bfloat16 [8192, 8192], P('wide', 'narrow'), as said below
- pattern: int32 [64, 64], P('wide', 'narrow'), may hold values from 0 to 1, as said below
- keep_mask: int32 [8192, 8192], P('wide', 'narrow'), may hold values 0 or 1
Outputs:
- clustered: float32 [8192, 8192], P('wide', 'narrow')
The draws below stay inside these ranges and needn't reach their ends.
Inputs may be any that keep to these rules, and one draw needn't show every extreme that they name: Each device's block of tiles holds between 1 and 6 tiles with pattern 1, and some device's block holds exactly 6. `values`: entries lie in a positive range.
All inputs are finite; a program needn't handle non-finite values. No bound on the sum of `keep_mask` on one device may be relied on, other than what follows from the above.
Results may differ from the reference program's by a relative error of at most 0.0003.
Values may be sent and summed in bfloat16 or wider, within the bound.
A program may use at most 256 MiB of HBM per device.

```python
import math
import jax
import jax.numpy as jnp

TILE = 128
ROWS_DEV = 256
KEEP = 6
N = 8192
N_WIDE = 32
N_NARROW = 8


def draw_values(key, part):
    key = jax.random.fold_in(key, 5)
    row_share = jnp.arange(N, dtype=jnp.float32)[:, None] / N
    base = jnp.exp(jax.random.uniform(key, (N, N), jnp.float32, math.log(0.05), 0.0))
    factor = 1.0 + 0.75 * row_share
    return (base * factor).astype(jnp.bfloat16)


def draw_pattern(key, part):
    key = jax.random.fold_in(key, 11)
    tile_rows = ROWS_DEV // TILE
    tile_cols = ROWS_DEV * N_WIDE // N_NARROW // TILE
    slots = tile_rows * tile_cols
    blocks = N_WIDE * N_NARROW
    first, second, third = jax.random.split(key, 3)
    counts = jax.random.randint(first, (blocks,), 1, KEEP + 1)
    fullest = jax.random.randint(second, (), 0, blocks)
    counts = jnp.where(jnp.arange(blocks) == fullest, KEEP, counts)
    scores = jax.random.randint(third, (blocks, slots), 0, 1 << 20) * slots + jnp.arange(slots)[None, :]
    ranks = jnp.argsort(jnp.argsort(scores, axis=1), axis=1)
    bits = (ranks < counts[:, None]).astype(jnp.int32)
    bits = bits.reshape(N_WIDE, N_NARROW, tile_rows, tile_cols).transpose(0, 2, 1, 3)
    return bits.reshape(N_WIDE * tile_rows, N_NARROW * tile_cols)


def plant(values, rng, smallest, largest):
    place = [jax.random.randint(jax.random.fold_in(rng, axis), (), 0, length) for axis, length in enumerate(values.shape)]
    main_axis = values.shape.index(max(values.shape))
    neighbour = place[:main_axis] + [(place[main_axis] + 1) % values.shape[main_axis]] + place[main_axis + 1:]
    return values.at[tuple(place)].set(smallest).at[tuple(neighbour)].set(largest)


def setup_inputs(seed: int = 0) -> dict:
    arg_keys = jax.random.split(jax.random.key(seed), 4)
    values = draw_values(jax.random.fold_in(arg_keys[3], 71), 0)
    pattern = draw_pattern(jax.random.fold_in(arg_keys[3], 71), 0)
    keep_mask = plant((jax.random.randint(arg_keys[2], (N, N), 0, 4) < 3).astype(jnp.int32), jax.random.fold_in(arg_keys[2], 1), 0, 1)
    return dict(values=values, pattern=pattern, keep_mask=keep_mask)


def reference(values, pattern, keep_mask):
    present = jnp.repeat(jnp.repeat(pattern, TILE, axis=0), TILE, axis=1)
    masked = jnp.where(present == 1, values, jnp.zeros_like(values))
    identity = jnp.eye(N, dtype=jnp.float32)
    matrix = (masked.astype(jnp.float32) + identity).astype(jnp.bfloat16)
    expanded = jnp.dot(matrix, matrix, preferred_element_type=jnp.float32)
    squared = expanded * expanded
    row_index = jnp.arange(N, dtype=jnp.int32)[:, None]
    col_index = jnp.arange(N, dtype=jnp.int32)[None, :]
    kept = (keep_mask == 1) | (row_index == col_index)
    pruned = jnp.where(kept, squared, jnp.zeros_like(squared))
    totals = jnp.sum(pruned, axis=0)
    return jnp.float32(N) * pruned / totals[None, :]
```

```python
import functools
import heapq

import jax
import jax.numpy as jnp
from jax import lax
from jax.experimental import pallas as pl
from jax.experimental.pallas import tpu as pltpu
from jax.sharding import PartitionSpec as P

TILE = 128
KEEP = 6
SLOTS = KEEP + 2
UNIT = 32
PART = TILE // UNIT
PACKED = KEEP * PART
NZ, NY, NX, NC = 8, 4, 4, 2
Z_UNITS = 14
MESH = pl.DeviceIdType.MESH


def ring_hops(n):
    full = (n - 1) // 2
    hops = []
    for step in (1, -1):
        for hop in range(full):
            hops.append(((-step * hop) % n, (-step * (hop + 1)) % n, step, None))
        if n % 2 == 0:
            half = 0 if step == 1 else 1
            hops.append(((-step * full) % n, (-step * (full + 1)) % n, step, half))
    return hops


def block_transfers():
    def rows(part, half):
        low, high = (0, Z_UNITS) if part == "z" else (Z_UNITS, PACKED)
        middle = (low + high) // 2
        return ((low, high), (low, middle), (middle, high))[0 if half is None else half + 1]

    found = []
    for a, b, step, half in ring_hops(NZ):
        found.append(("z", "z", step, (0, a), (0, b), rows("z", half)))
    for a, b, step, half in ring_hops(NY):
        found.append(("y", "y", step, (a, 0), (b, 0), rows("y", half)))
    for dz in range(NZ):
        for a, b, step, half in ring_hops(NY):
            found.append(("z", "y", step, (a, dz), (b, dz), rows("z", half)))
    for dy in range(NY):
        for a, b, step, half in ring_hops(NZ):
            found.append(("y", "z", step, (dy, a), (dy, b), rows("y", half)))
    return found


def plan(transfers, rate=46e3, latency=1.0):
    have = {("z", 0, 0): [(0, Z_UNITS)], ("y", 0, 0): [(Z_UNITS, PACKED)]}
    waiting = list(range(len(transfers)))
    queues, free, events = {}, {}, []
    arrivals, released = [], {-1: []}

    def ready(index):
        part, _, _, (dy, dz), _, (low, high) = transfers[index]
        for a, b in sorted(have.get((part, dy, dz), [])):
            if a <= low < b:
                low = b
        return low >= high

    def pump(now, cause):
        for index in [i for i in waiting if ready(i)]:
            waiting.remove(index)
            queues.setdefault(transfers[index][1:3], []).append(index)
            released[cause].append(index)
        for link, queue in queues.items():
            if queue and free.get(link, 0.0) <= now:
                queue.sort(key=lambda i: (transfers[i][0] != link[0], i))
                index = queue.pop(0)
                low, high = transfers[index][5]
                took = (high - low) * UNIT * TILE * 2 / rate
                free[link] = now + took
                heapq.heappush(events, (now + took, -1))
                heapq.heappush(events, (now + took + latency, index))

    pump(0.0, -1)
    while events:
        now, index = heapq.heappop(events)
        if index >= 0:
            part, _, _, _, (dy, dz), rows = transfers[index]
            have.setdefault((part, dy, dz), []).append(rows)
            arrivals.append((now, index))
            released[index] = []
        pump(now, index)
    return arrivals, released


def kernel(
    col_tiles,
    pattern_s,
    values,
    keep,
    out,
    held,
    slab,
    dense,
    acc,
    keep_v,
    tiles,
    meta_b,
    meta_a,
    meta_v,
    meta_s,
    tot_y,
    tot_z,
    send_sem,
    recv_sem,
    side_send,
    side_recv,
    small_send,
    small_recv,
    local_sem,
):
    wide, narrow = lax.axis_index("wide"), lax.axis_index("narrow")
    z, y = wide // NY, wide % NY
    x, core = narrow // NC, narrow % NC
    blocks = NX * NC

    def at(dy=0, dz=0):
        return (lax.rem(z + dz, NZ) * NY + lax.rem(y + dy, NY), narrow)

    def beside(dx, dc):
        return (wide, lax.rem(x + dx, NX) * NC + lax.rem(core + dc, NC))

    def remote(src, dst, send, recv, device):
        return pltpu.make_async_remote_copy(
            src_ref=src, dst_ref=dst, send_sem=send, recv_sem=recv, device_id=device, device_id_type=MESH
        )

    keep_copy = pltpu.make_async_copy(keep, keep_v, local_sem.at[0])
    keep_copy.start()

    z_peers = list(range(1, NZ))
    y_peers = list(range(1, NY))
    narrow_peers = [(dx, dc) for dx in range(NX) for dc in range(NC) if (dx, dc) != (0, 0)]
    peers = [at(dz=d) for d in z_peers] + [at(dy=d) for d in y_peers] + [beside(*d) for d in narrow_peers]
    barrier = pltpu.get_barrier_semaphore()
    for peer in peers:
        pl.semaphore_signal(barrier, inc=1, device_id=peer, device_id_type=MESH)

    eye = (
        lax.broadcasted_iota(jnp.int32, (TILE, TILE), 0) == lax.broadcasted_iota(jnp.int32, (TILE, TILE), 1)
    ).astype(jnp.float32)
    lane = lax.broadcasted_iota(jnp.int32, (8, TILE), 1)
    def same(a, b):
        return jnp.maximum(0, 1 - jnp.maximum(a - b, b - a))

    zero = jnp.int32(0)
    filled = zero
    picked = [zero] * KEEP
    codes = jnp.zeros((8, TILE), jnp.int32)
    for r in range(2):
        for c in range(col_tiles):
            present = pattern_s[r, c]
            diagonal = jnp.where(2 * wide + r == col_tiles * narrow + c, 1, 0)
            code = present * filled + (1 - present) * (KEEP + diagonal)
            codes = jnp.where(lane == r * col_tiles + c, code, codes)
            for s in range(KEEP):
                mine = present * same(filled, s)
                picked[s] += mine * (r * col_tiles + c)
            filled = filled + present
            tiles[r * col_tiles + c] = values[r * TILE : (r + 1) * TILE, c * TILE : (c + 1) * TILE]
    shift = 2 * TILE * wide - col_tiles * TILE * narrow
    corner = 2 * wide - col_tiles * narrow
    for s, position in enumerate(picked):
        on = same(position, corner) + same(position, corner + 1 + col_tiles)
        inside = jnp.where(jnp.logical_and(corner >= 0, corner < col_tiles), 1, 0)
        on = (on * inside).astype(jnp.float32)
        tile = (tiles[position].astype(jnp.float32) + on * eye).astype(jnp.bfloat16)
        tile = tile.reshape(PART, UNIT, TILE)
        slab[narrow, s * PART : (s + 1) * PART] = tile
        held[0][y, s * PART : (s + 1) * PART] = tile
    meta_b[0, 0] = codes
    meta_a[narrow] = codes

    pl.semaphore_wait(barrier, len(peers))

    transfers = block_transfers()
    arrivals, released = plan(transfers)

    def block_copy(index):
        _, axis, step, (dy, dz), (_, dz_there), (low, high) = transfers[index]
        row = lax.rem(y + dy, NY)
        device = at(dz=step % NZ) if axis == "z" else at(dy=step % NY)
        window = pl.ds(low, high - low)
        return remote(
            held[dz].at[row, window],
            held[dz_there].at[row, window],
            send_sem.at[index],
            recv_sem.at[index],
            device,
        )

    def block_arrival(index):
        _, axis, step, _, (dy, dz), (low, high) = transfers[index]
        device = at(dz=step % NZ) if axis == "z" else at(dy=step % NY)
        here = held[dz].at[lax.rem(y + dy, NY), pl.ds(low, high - low)]
        return remote(here, here, send_sem.at[index], recv_sem.at[index], device)

    sent = []

    def start(copy):
        copy.start()
        sent.append(copy)

    for index in released[-1]:
        start(block_copy(index))

    def side_copy(index, block, device):
        ref = slab.at[block, pl.ds(0, PACKED)]
        return remote(ref, ref, side_send.at[index], side_recv.at[index], device)

    along_x = list(range(1, NX))
    for dx in along_x:
        start(side_copy(dx, narrow, beside(dx, 0)))
    start(side_copy(0, narrow, beside(0, 1)))

    for k, d in enumerate(z_peers):
        start(remote(meta_b.at[0, 0], meta_b.at[0, NZ - d], small_send.at[k], small_recv.at[k], at(dz=d)))
    first_narrow = len(z_peers)
    for k, (dx, dc) in enumerate(narrow_peers):
        k += first_narrow
        start(remote(meta_a.at[narrow], meta_a.at[narrow], small_send.at[k], small_recv.at[k], beside(dx, dc)))
    first_y = first_narrow + len(narrow_peers)
    first_total = first_y + len(y_peers)

    blank = jnp.zeros((PART, UNIT, TILE), jnp.bfloat16)
    unit = eye.astype(jnp.bfloat16).reshape(PART, UNIT, TILE)
    for ref, count in [(slab, blocks)] + [(ref, NY) for ref in held]:
        for i in range(count):
            ref[i, PACKED : PACKED + PART] = blank
            ref[i, PACKED + PART : PACKED + 2 * PART] = unit

    def meta_along_y():
        for k, d in enumerate(z_peers):
            here = meta_b.at[0, NZ - d]
            remote(here, here, small_send.at[k], small_recv.at[k], at(dz=d)).wait_recv()
        for k, d in enumerate(y_peers):
            k += first_y
            start(remote(meta_b.at[0], meta_b.at[NY - d], small_send.at[k], small_recv.at[k], at(dy=d)))

    def meta_to_scalars():
        for k, (dx, dc) in enumerate(narrow_peers):
            k += first_narrow
            here = meta_a.at[lax.rem(x + NX - dx, NX) * NC + lax.rem(core + NC - dc, NC)]
            remote(here, here, small_send.at[k], small_recv.at[k], beside(dx, dc)).wait_recv()
        for k, d in enumerate(y_peers):
            k += first_y
            here = meta_b.at[NY - d]
            remote(here, here, small_send.at[k], small_recv.at[k], at(dy=d)).wait_recv()
        for dz in range(NZ):
            for dy in range(NY):
                row = dz * NY + dy
                meta_v[row : row + 1, :] = meta_b[dy, dz, 0:1, :]
        for n in range(blocks):
            row = NZ * NY + n
            meta_v[row : row + 1, :] = meta_a[n, 0:1, :]
        copy = pltpu.make_async_copy(meta_v, meta_s, local_sem.at[1])
        copy.start()
        copy.wait()

    def side_arrivals():
        for dx in along_x:
            source = lax.rem(x + NX - dx, NX) * NC + core
            side_copy(dx, source, beside(dx, 0)).wait_recv()
            start(side_copy(NX - 1 + dx, source, beside(0, 1)))

    def tile_of(ref, block, code):
        return ref[block, pl.ds(code * PART, PART)].reshape(TILE, TILE)

    def expand_slab():
        side_copy(0, lax.rem(x, NX) * NC + lax.rem(core + 1, NC), beside(0, 1)).wait_recv()
        for dx in along_x:
            source = lax.rem(x + NX - dx, NX) * NC + lax.rem(core + 1, NC)
            side_copy(NX - 1 + dx, source, beside(0, 1)).wait_recv()

        def body(n, carry):
            for r in range(2):
                for c in range(col_tiles):
                    code = meta_s[NZ * NY + n, r * col_tiles + c]
                    dense[n, r * TILE : (r + 1) * TILE, c * TILE : (c + 1) * TILE] = tile_of(slab, n, code)
            return carry

        lax.fori_loop(0, blocks, body, 0)

    def multiply(dz, first):
        lhs_index = lax.rem(z + dz, NZ)

        def body(pair, carry):
            strips = []
            for row in range(NY):
                meta_row = dz * NY + lax.rem(row - y + NY, NY)
                for r in range(2):
                    tiles = []
                    for c in range(2):
                        code = meta_s[meta_row, r * col_tiles + pair * 2 + c]
                        tiles.append(tile_of(held[dz], row, code))
                    strips.append(jnp.concatenate(tiles, axis=1))
            product = jnp.dot(
                dense[lhs_index], jnp.concatenate(strips, axis=0), preferred_element_type=jnp.float32
            )
            columns = pl.ds(pl.multiple_of(pair * 2 * TILE, 2 * TILE), 2 * TILE)
            if first:
                acc[:, columns] = product
            else:
                acc[:, columns] += product
            return carry

        lax.fori_loop(0, col_tiles // 2, body, 0)

    extras = [(3.0, meta_along_y), (6.0, meta_to_scalars), (7.0, side_arrivals), (10.0, expand_slab)]
    left = {}
    for _, index in arrivals:
        dz = transfers[index][4][1]
        left[dz] = left.get(dz, 0) + 1
    done = []
    expanded = False

    def run_extras(now):
        nonlocal expanded
        while extras and extras[0][0] <= now:
            _, action = extras.pop(0)
            action()
            expanded = action is expand_slab
        if expanded:
            while done:
                dz = done.pop(0)
                multiply(dz, not multiplied)
                multiplied.append(dz)

    multiplied = []
    for now, index in arrivals:
        run_extras(now)
        block_arrival(index).wait_recv()
        for following in released[index]:
            start(block_copy(following))
        dz = transfers[index][4][1]
        left[dz] -= 1
        if left[dz] == 0:
            done.append(dz)
    run_extras(float("inf"))

    keep_copy.wait()
    row_id = lax.broadcasted_iota(jnp.int32, (2 * TILE, TILE), 0)
    col_id = lax.broadcasted_iota(jnp.int32, (2 * TILE, TILE), 1)
    if col_tiles < 8:
        tot_y[0] = jnp.ones((8, TILE), jnp.float32)
    for c in range(col_tiles):
        columns = slice(c * TILE, (c + 1) * TILE)
        expanded_tile = acc[:, columns]
        kept = jnp.logical_or(keep_v[:, columns] == 1, row_id + shift == col_id + c * TILE)
        pruned = jnp.where(kept, expanded_tile * expanded_tile, 0.0)
        out[:, columns] = pruned
        tot_y[0, c : c + 1, :] = jnp.sum(pruned, axis=0, keepdims=True)

    for k, d in enumerate(y_peers):
        k += first_total
        start(remote(tot_y.at[0], tot_y.at[NY - d], small_send.at[k], small_recv.at[k], at(dy=d)))
    for k, d in enumerate(y_peers):
        k += first_total
        here = tot_y.at[NY - d]
        remote(here, here, small_send.at[k], small_recv.at[k], at(dy=d)).wait_recv()
    tot_z[0] = functools.reduce(jnp.add, [tot_y[d] for d in range(NY)])
    first_total_z = first_total + len(y_peers)
    for k, d in enumerate(z_peers):
        k += first_total_z
        start(remote(tot_z.at[0], tot_z.at[NZ - d], small_send.at[k], small_recv.at[k], at(dz=d)))
    for k, d in enumerate(z_peers):
        k += first_total_z
        here = tot_z.at[NZ - d]
        remote(here, here, small_send.at[k], small_recv.at[k], at(dz=d)).wait_recv()
    total = functools.reduce(jnp.add, [tot_z[d] for d in range(NZ)])
    scale = (2 * TILE * NZ * NY) / total
    for c in range(col_tiles):
        columns = slice(c * TILE, (c + 1) * TILE)
        out[:, columns] = out[:, columns] * scale[c : c + 1, :]

    for copy in sent:
        copy.wait_send()


def shards(values, pattern, keep_mask):
    rows, cols = values.shape
    col_tiles = cols // TILE
    blocks = NX * NC
    transfers = len(block_transfers())
    small = 2 * (NZ - 1) + 2 * (NY - 1) + blocks - 1
    return pl.pallas_call(
        functools.partial(kernel, col_tiles),
        out_shape=jax.ShapeDtypeStruct((rows, cols), jnp.float32),
        in_specs=[
            pl.BlockSpec(memory_space=pltpu.SMEM),
            pl.BlockSpec(memory_space=pltpu.VMEM),
            pl.BlockSpec(memory_space=pl.ANY),
        ],
        out_specs=pl.BlockSpec(memory_space=pltpu.VMEM),
        scratch_shapes=[
            [pltpu.VMEM((NY, SLOTS * PART, UNIT, TILE), jnp.bfloat16) for _ in range(NZ)],
            pltpu.VMEM((blocks, SLOTS * PART, UNIT, TILE), jnp.bfloat16),
            pltpu.VMEM((blocks, rows, cols), jnp.bfloat16),
            pltpu.VMEM((rows, cols), jnp.float32),
            pltpu.VMEM((rows, cols), jnp.int32),
            pltpu.VMEM((2 * col_tiles, TILE, TILE), jnp.bfloat16),
            pltpu.VMEM((NY, NZ, 8, TILE), jnp.int32),
            pltpu.VMEM((blocks, 8, TILE), jnp.int32),
            pltpu.VMEM((NZ * NY + blocks, TILE), jnp.int32),
            pltpu.SMEM((NZ * NY + blocks, TILE), jnp.int32),
            pltpu.VMEM((NY, 8, TILE), jnp.float32),
            pltpu.VMEM((NZ, 8, TILE), jnp.float32),
            pltpu.SemaphoreType.DMA((transfers,)),
            pltpu.SemaphoreType.DMA((transfers,)),
            pltpu.SemaphoreType.DMA((2 * NX - 1,)),
            pltpu.SemaphoreType.DMA((2 * NX - 1,)),
            pltpu.SemaphoreType.DMA((small,)),
            pltpu.SemaphoreType.DMA((small,)),
            pltpu.SemaphoreType.DMA((2,)),
        ],
        compiler_params=pltpu.CompilerParams(
            collective_id=0, has_side_effects=True, vmem_limit_bytes=48 * 1024 * 1024
        ),
        cost_estimate=pl.CostEstimate(flops=2 * rows * cols * 8192, bytes_accessed=12 << 20, transcendentals=0),
    )(pattern, values, keep_mask)


def solution(mesh):
    return jax.shard_map(
        shards,
        mesh=mesh,
        in_specs=(P("wide", "narrow"), P("wide", "narrow"), P("wide", "narrow")),
        out_specs=P("wide", "narrow"),
        check_vma=False,
    )
```

```python
import functools
import heapq

import jax
import jax.numpy as jnp
from jax import lax
from jax.experimental import pallas as pl
from jax.experimental.pallas import tpu as pltpu
from jax.sharding import PartitionSpec as P

TILE = 128
KEEP = 6
SLOTS = KEEP + 2
UNIT = 32
PART = TILE // UNIT
PACKED = KEEP * PART
NZ, NY, NX, NC = 8, 4, 4, 2
LEAD = 1.0
Z_UNITS = 14
MESH = pl.DeviceIdType.MESH


def ring_hops(n):
    full = (n - 1) // 2
    hops = []
    for step in (1, -1):
        for hop in range(full):
            hops.append(((-step * hop) % n, (-step * (hop + 1)) % n, step, None))
        if n % 2 == 0:
            half = 0 if step == 1 else 1
            hops.append(((-step * full) % n, (-step * (full + 1)) % n, step, half))
    return hops


def block_transfers():
    def rows(part, half):
        low, high = (0, Z_UNITS) if part == "z" else (Z_UNITS, PACKED)
        middle = (low + high) // 2
        return ((low, high), (low, middle), (middle, high))[0 if half is None else half + 1]

    found = []
    for a, b, step, half in ring_hops(NZ):
        found.append(("z", "z", step, (0, a), (0, b), rows("z", half)))
    for a, b, step, half in ring_hops(NY):
        found.append(("y", "y", step, (a, 0), (b, 0), rows("y", half)))
    for dz in range(NZ):
        for a, b, step, half in ring_hops(NY):
            found.append(("z", "y", step, (a, dz), (b, dz), rows("z", half)))
    for dy in range(NY):
        for a, b, step, half in ring_hops(NZ):
            found.append(("y", "z", step, (dy, a), (dy, b), rows("y", half)))
    return found


def plan(transfers, rate=46e3, latency=2.5):
    have = {("z", 0, 0): [(0, Z_UNITS)], ("y", 0, 0): [(Z_UNITS, PACKED)]}
    waiting = list(range(len(transfers)))
    queues, free, events = {}, {}, []
    arrivals, starts, cause_of = [], {}, {}

    def ready(index):
        part, _, _, (dy, dz), _, (low, high) = transfers[index]
        for a, b in sorted(have.get((part, dy, dz), [])):
            if a <= low < b:
                low = b
        return low >= high

    def pump(now, cause):
        for index in [i for i in waiting if ready(i)]:
            waiting.remove(index)
            queues.setdefault(transfers[index][1:3], []).append(index)
            cause_of[index] = cause
        for link, queue in queues.items():
            if queue and free.get(link, 0.0) <= now:
                queue.sort(key=lambda i: (transfers[i][0] != link[0], i))
                index = queue.pop(0)
                low, high = transfers[index][5]
                took = (high - low) * UNIT * TILE * 2 / rate
                free[link] = now + took
                starts[index] = now
                heapq.heappush(events, (now + took, -1))
                heapq.heappush(events, (now + took + latency, index))

    pump(0.0, -1)
    while events:
        now, index = heapq.heappop(events)
        if index >= 0:
            part, _, _, _, (dy, dz), rows = transfers[index]
            have.setdefault((part, dy, dz), []).append(rows)
            arrivals.append((now, index))
        pump(now, index)
    arrived_at = {index: now for now, index in arrivals}
    released = {-1: []}
    for index in sorted(starts, key=lambda i: (starts[i], i)):
        cause = cause_of[index]
        for now, earlier in arrivals:
            if now > starts[index] - LEAD:
                break
            if cause == -1 or now > arrived_at[cause]:
                cause = earlier
        released.setdefault(cause, []).append(index)
    return arrivals, released


def kernel(
    col_tiles,
    pattern,
    values,
    keep,
    out,
    held,
    last,
    slab,
    dense,
    keep_v,
    pattern_s,
    tiles,
    meta_b,
    meta_a,
    meta_v,
    meta_s,
    tot_y,
    tot_z,
    send_sem,
    recv_sem,
    side_send,
    side_recv,
    small_send,
    small_recv,
    local_sem,
):
    wide, narrow = lax.axis_index("wide"), lax.axis_index("narrow")
    z, y = wide // NY, wide % NY
    x, core = narrow // NC, narrow % NC
    blocks = NX * NC

    def at(dy=0, dz=0):
        return (lax.rem(z + dz, NZ) * NY + lax.rem(y + dy, NY), narrow)

    def beside(dx, dc):
        return (wide, lax.rem(x + dx, NX) * NC + lax.rem(core + dc, NC))

    def remote(src, dst, send, recv, device):
        return pltpu.make_async_remote_copy(
            src_ref=src, dst_ref=dst, send_sem=send, recv_sem=recv, device_id=device, device_id_type=MESH
        )

    pattern_copy = pltpu.make_async_copy(pattern, pattern_s, local_sem.at[2])
    pattern_copy.start()
    tile_copies = []
    for r in range(2):
        for c in range(col_tiles):
            source = values.at[pl.ds(r * TILE, TILE), pl.ds(c * TILE, TILE)]
            p = r * col_tiles + c
            tile_copies.append(pltpu.make_async_copy(source, tiles.at[p], local_sem.at[3 + p]))
            tile_copies[p].start()
    keep_copy = pltpu.make_async_copy(keep, keep_v, local_sem.at[0])
    keep_copy.start()

    z_peers = list(range(1, NZ))
    y_peers = list(range(1, NY))
    narrow_peers = [(dx, dc) for dx in range(NX) for dc in range(NC) if (dx, dc) != (0, 0)]
    peers = [at(dz=d) for d in z_peers] + [at(dy=d) for d in y_peers] + [beside(*d) for d in narrow_peers]
    barrier = pltpu.get_barrier_semaphore()
    for peer in peers:
        pl.semaphore_signal(barrier, inc=1, device_id=peer, device_id_type=MESH)

    eye = (
        lax.broadcasted_iota(jnp.int32, (TILE, TILE), 0) == lax.broadcasted_iota(jnp.int32, (TILE, TILE), 1)
    ).astype(jnp.float32)
    lane = lax.broadcasted_iota(jnp.int32, (8, TILE), 1)
    def same(a, b):
        return jnp.maximum(0, 1 - jnp.maximum(a - b, b - a))

    zero = jnp.int32(0)
    filled = zero
    picked = [zero] * KEEP
    pattern_copy.wait()
    codes = jnp.zeros((8, TILE), jnp.int32)
    for r in range(2):
        for c in range(col_tiles):
            present = pattern_s[r, c]
            diagonal = jnp.where(2 * wide + r == col_tiles * narrow + c, 1, 0)
            code = present * filled + (1 - present) * (KEEP + diagonal)
            codes = jnp.where(lane == r * col_tiles + c, code, codes)
            for s in range(KEEP):
                mine = present * same(filled, s)
                picked[s] += mine * (r * col_tiles + c)
            filled = filled + present
    shift = 2 * TILE * wide - col_tiles * TILE * narrow
    corner = 2 * wide - col_tiles * narrow
    for copy in tile_copies:
        copy.wait()
    for s, position in enumerate(picked):
        on = same(position, corner) + same(position, corner + 1 + col_tiles)
        inside = jnp.where(jnp.logical_and(corner >= 0, corner < col_tiles), 1, 0)
        on = (on * inside).astype(jnp.float32)
        tile = (tiles[position].astype(jnp.float32) + on * eye).astype(jnp.bfloat16)
        tile = tile.reshape(PART, UNIT, TILE)
        slab[narrow, s * PART : (s + 1) * PART] = tile
        held[0][y, s * PART : (s + 1) * PART] = tile
    meta_b[0, 0] = codes
    meta_a[narrow] = codes

    pl.semaphore_wait(barrier, len(peers))

    transfers = block_transfers()
    arrivals, released = plan(transfers)
    final = transfers[arrivals[-1][1]][4][1]

    def place(dy, dz):
        return last[dy].at[0] if dz == final else held[dz].at[lax.rem(y + dy, NY)]


    def block_copy(index):
        _, axis, step, there, here, (low, high) = transfers[index]
        device = at(dz=step % NZ) if axis == "z" else at(dy=step % NY)
        window = pl.ds(low, high - low)
        if here[1] == final:
            target = last[here[0]].at[0]
        else:
            target = held[here[1]].at[lax.rem(y + there[0], NY)]
        return remote(
            place(*there).at[window], target.at[window], send_sem.at[index], recv_sem.at[index], device
        )

    def block_arrival(index):
        _, axis, step, _, (dy, dz), (low, high) = transfers[index]
        device = at(dz=step % NZ) if axis == "z" else at(dy=step % NY)
        here = place(dy, dz).at[pl.ds(low, high - low)]
        return remote(here, here, send_sem.at[index], recv_sem.at[index], device)

    sent = []

    def start(copy):
        copy.start()
        sent.append(copy)

    for index in released[-1]:
        start(block_copy(index))

    def side_copy(index, block, device):
        ref = slab.at[block, pl.ds(0, PACKED)]
        return remote(ref, ref, side_send.at[index], side_recv.at[index], device)

    along_x = list(range(1, NX))
    for dx in along_x:
        start(side_copy(dx, narrow, beside(dx, 0)))
    start(side_copy(0, narrow, beside(0, 1)))

    for k, d in enumerate(z_peers):
        start(remote(meta_b.at[0, 0], meta_b.at[0, NZ - d], small_send.at[k], small_recv.at[k], at(dz=d)))
    first_narrow = len(z_peers)
    for k, (dx, dc) in enumerate(narrow_peers):
        k += first_narrow
        start(remote(meta_a.at[narrow], meta_a.at[narrow], small_send.at[k], small_recv.at[k], beside(dx, dc)))
    first_y = first_narrow + len(narrow_peers)
    first_total = first_y + len(y_peers)

    blank = jnp.zeros((PART, UNIT, TILE), jnp.bfloat16)
    unit = eye.astype(jnp.bfloat16).reshape(PART, UNIT, TILE)
    for ref, count in [(slab, blocks)] + [(held[dz], NY) for dz in range(NZ) if dz != final] + [(ref, 1) for ref in last]:
        for i in range(count):
            ref[i, PACKED : PACKED + PART] = blank
            ref[i, PACKED + PART : PACKED + 2 * PART] = unit

    def meta_along_y():
        for k, d in enumerate(z_peers):
            here = meta_b.at[0, NZ - d]
            remote(here, here, small_send.at[k], small_recv.at[k], at(dz=d)).wait_recv()
        for k, d in enumerate(y_peers):
            k += first_y
            start(remote(meta_b.at[0], meta_b.at[NY - d], small_send.at[k], small_recv.at[k], at(dy=d)))

    def meta_to_scalars():
        for k, (dx, dc) in enumerate(narrow_peers):
            k += first_narrow
            here = meta_a.at[lax.rem(x + NX - dx, NX) * NC + lax.rem(core + NC - dc, NC)]
            remote(here, here, small_send.at[k], small_recv.at[k], beside(dx, dc)).wait_recv()
        for k, d in enumerate(y_peers):
            k += first_y
            here = meta_b.at[NY - d]
            remote(here, here, small_send.at[k], small_recv.at[k], at(dy=d)).wait_recv()
        for dz in range(NZ):
            for dy in range(NY):
                row = dz * NY + dy
                meta_v[row : row + 1, :] = meta_b[dy, dz, 0:1, :]
        for n in range(blocks):
            row = NZ * NY + n
            meta_v[row : row + 1, :] = meta_a[n, 0:1, :]
        copy = pltpu.make_async_copy(meta_v, meta_s, local_sem.at[1])
        copy.start()
        copy.wait()

    def side_arrivals():
        for dx in along_x:
            source = lax.rem(x + NX - dx, NX) * NC + core
            side_copy(dx, source, beside(dx, 0)).wait_recv()
            start(side_copy(NX - 1 + dx, source, beside(0, 1)))

    def tile_of(ref, block, code):
        return ref[block, pl.ds(code * PART, PART)].reshape(TILE, TILE)

    def expand_slab():
        side_copy(0, lax.rem(x, NX) * NC + lax.rem(core + 1, NC), beside(0, 1)).wait_recv()
        for dx in along_x:
            source = lax.rem(x + NX - dx, NX) * NC + lax.rem(core + 1, NC)
            side_copy(NX - 1 + dx, source, beside(0, 1)).wait_recv()

        def body(n, carry):
            for r in range(2):
                for c in range(col_tiles):
                    code = meta_s[NZ * NY + n, r * col_tiles + c]
                    dense[n, r * TILE : (r + 1) * TILE, c * TILE : (c + 1) * TILE] = tile_of(slab, n, code)
            return carry

        lax.fori_loop(0, blocks, body, 0)

    row_id = lax.broadcasted_iota(jnp.int32, (2 * TILE, TILE), 0)
    col_id = lax.broadcasted_iota(jnp.int32, (2 * TILE, TILE), 1)

    def strip(ref, row, dy, dz, pair):
        halves = []
        for r in range(2):
            codes = [meta_s[dz * NY + dy, r * col_tiles + pair * 2 + c] for c in range(2)]
            halves.append(jnp.concatenate([tile_of(ref, row, code) for code in codes], axis=1))
        return halves

    def multiply_plane(dz, pair, first):
        halves = []
        for row in range(NY):
            halves += strip(held[dz], row, lax.rem(row - y + NY, NY), dz, pair)
        product = jnp.dot(
            dense[lax.rem(z + dz, NZ)], jnp.concatenate(halves, axis=0), preferred_element_type=jnp.float32
        )
        columns = slice(pair * 2 * TILE, (pair + 1) * 2 * TILE)
        if first:
            out[:, columns] = product
        else:
            out[:, columns] += product

    def multiply_block(dy, pair, finish):
        depth = pl.ds(pl.multiple_of(lax.rem(y + dy, NY) * 2 * TILE, 2 * TILE), 2 * TILE)
        rhs = jnp.concatenate(strip(last[dy], 0, dy, final, pair), axis=0)
        product = jnp.dot(dense[lax.rem(z + final, NZ), :, depth], rhs, preferred_element_type=jnp.float32)
        columns = slice(pair * 2 * TILE, (pair + 1) * 2 * TILE)
        if not finish:
            out[:, columns] += product
            return
        product = out[:, columns] + product
        for half in range(2):
            c = pair * 2 + half
            columns = slice(c * TILE, (c + 1) * TILE)
            value = product[:, half * TILE : (half + 1) * TILE]
            kept = jnp.logical_or(keep_v[:, columns] == 1, row_id + shift == col_id + c * TILE)
            pruned = jnp.where(kept, value * value, 0.0)
            out[:, columns] = pruned
            tot_y[0, c : c + 1, :] = jnp.sum(pruned, axis=0, keepdims=True)

    extras = [(8.0, meta_along_y), (10.0, side_arrivals), (14.0, meta_to_scalars), (15.0, expand_slab)]
    pairs = col_tiles // 2
    left = {}

    def unit_of(index):
        dy, dz = transfers[index][4]
        return (dy, dz) if dz == final else (None, dz)

    for _, index in arrivals:
        left[unit_of(index)] = left.get(unit_of(index), 0) + 1
    blocks_left = NY
    queue, multiplied = [], []
    clock = 0.0

    def run(budget):
        nonlocal clock
        while queue and extras == [] and clock + queue[0][0] <= budget:
            cost, action = queue.pop(0)
            action()
            clock += cost

    for now, index in arrivals:
        end = index == arrivals[-1][1]
        while extras and (end or extras[0][0] <= now):
            extras.pop(0)[1]()
        run(float("inf") if end else now)
        block_arrival(index).wait_recv()
        clock = max(clock, now)
        for following in released.get(index, []):
            start(block_copy(following))
        left[unit_of(index)] -= 1
        if left[unit_of(index)] == 0:
            dy, dz = unit_of(index)
            for pair in range(pairs):
                if dy is None:
                    queue.append((0.3, functools.partial(multiply_plane, dz, pair, not multiplied)))
                else:
                    queue.append((0.1, functools.partial(multiply_block, dy, pair, blocks_left == 1)))
            if dy is None:
                multiplied.append(dz)
            else:
                blocks_left -= 1
    keep_copy.wait()
    if col_tiles < 8:
        tot_y[0] = jnp.ones((8, TILE), jnp.float32)
    run(float("inf"))

    for k, d in enumerate(y_peers):
        k += first_total
        start(remote(tot_y.at[0], tot_y.at[NY - d], small_send.at[k], small_recv.at[k], at(dy=d)))
    settled = len(sent) - len(y_peers)
    for copy in sent[:settled]:
        copy.wait_send()
    for k, d in enumerate(y_peers):
        k += first_total
        here = tot_y.at[NY - d]
        remote(here, here, small_send.at[k], small_recv.at[k], at(dy=d)).wait_recv()
    tot_z[0] = functools.reduce(jnp.add, [tot_y[d] for d in range(NY)])
    first_total_z = first_total + len(y_peers)
    for k, d in enumerate(z_peers):
        k += first_total_z
        start(remote(tot_z.at[0], tot_z.at[NZ - d], small_send.at[k], small_recv.at[k], at(dz=d)))
    for k, d in enumerate(z_peers):
        k += first_total_z
        here = tot_z.at[NZ - d]
        remote(here, here, small_send.at[k], small_recv.at[k], at(dz=d)).wait_recv()
    total = functools.reduce(jnp.add, [tot_z[d] for d in range(NZ)])
    scale = (2 * TILE * NZ * NY) / total
    for c in range(col_tiles):
        columns = slice(c * TILE, (c + 1) * TILE)
        out[:, columns] = out[:, columns] * scale[c : c + 1, :]
    for copy in sent[settled:]:
        copy.wait_send()


def shards(values, pattern, keep_mask):
    rows, cols = values.shape
    col_tiles = cols // TILE
    blocks = NX * NC
    transfers = len(block_transfers())
    small = 2 * (NZ - 1) + 2 * (NY - 1) + blocks - 1
    return pl.pallas_call(
        functools.partial(kernel, col_tiles),
        out_shape=jax.ShapeDtypeStruct((rows, cols), jnp.float32),
        in_specs=[
            pl.BlockSpec(memory_space=pltpu.HBM),
            pl.BlockSpec(memory_space=pltpu.HBM),
            pl.BlockSpec(memory_space=pltpu.HBM),
        ],
        out_specs=pl.BlockSpec(memory_space=pltpu.VMEM),
        scratch_shapes=[
            [pltpu.VMEM((NY, SLOTS * PART, UNIT, TILE), jnp.bfloat16) for _ in range(NZ)],
            [pltpu.VMEM((1, SLOTS * PART, UNIT, TILE), jnp.bfloat16) for _ in range(NY)],
            pltpu.VMEM((blocks, SLOTS * PART, UNIT, TILE), jnp.bfloat16),
            pltpu.VMEM((blocks, rows, cols), jnp.bfloat16),
            pltpu.VMEM((rows, cols), jnp.int32),
            pltpu.SMEM((2, col_tiles), jnp.int32),
            pltpu.VMEM((2 * col_tiles, TILE, TILE), jnp.bfloat16),
            pltpu.VMEM((NY, NZ, 8, TILE), jnp.int32),
            pltpu.VMEM((blocks, 8, TILE), jnp.int32),
            pltpu.VMEM((NZ * NY + blocks, TILE), jnp.int32),
            pltpu.SMEM((NZ * NY + blocks, TILE), jnp.int32),
            pltpu.VMEM((NY, 8, TILE), jnp.float32),
            pltpu.VMEM((NZ, 8, TILE), jnp.float32),
            pltpu.SemaphoreType.DMA((transfers,)),
            pltpu.SemaphoreType.DMA((transfers,)),
            pltpu.SemaphoreType.DMA((2 * NX - 1,)),
            pltpu.SemaphoreType.DMA((2 * NX - 1,)),
            pltpu.SemaphoreType.DMA((small,)),
            pltpu.SemaphoreType.DMA((small,)),
            pltpu.SemaphoreType.DMA((3 + 2 * col_tiles,)),
        ],
        compiler_params=pltpu.CompilerParams(
            collective_id=0, has_side_effects=True, vmem_limit_bytes=52 * 1024 * 1024
        ),
        cost_estimate=pl.CostEstimate(flops=2 * rows * cols * 8192, bytes_accessed=12 << 20, transcendentals=0),
    )(pattern, values, keep_mask)


def solution(mesh):
    return jax.shard_map(
        shards,
        mesh=mesh,
        in_specs=(P("wide", "narrow"), P("wide", "narrow"), P("wide", "narrow")),
        out_specs=P("wide", "narrow"),
        check_vma=False,
    )
```

```python
import functools
import heapq

import jax
import jax.numpy as jnp
from jax import lax
from jax.experimental import pallas as pl
from jax.experimental.pallas import tpu as pltpu
from jax.sharding import PartitionSpec as P

TILE = 128
KEEP = 6
SLOTS = KEEP + 2
UNIT = 32
PART = TILE // UNIT
PACKED = KEEP * PART
NZ, NY, NX, NC = 8, 4, 4, 2
RETIRE = 20
LEAD = 1.0
Z_UNITS = 14
MESH = pl.DeviceIdType.MESH


def ring_hops(n):
    full = (n - 1) // 2
    hops = []
    for step in (1, -1):
        for hop in range(full):
            hops.append(((-step * hop) % n, (-step * (hop + 1)) % n, step, None))
        if n % 2 == 0:
            half = 0 if step == 1 else 1
            hops.append(((-step * full) % n, (-step * (full + 1)) % n, step, half))
    return hops


def block_transfers():
    def rows(part, half):
        low, high = (0, Z_UNITS) if part == "z" else (Z_UNITS, PACKED)
        middle = (low + high) // 2
        return ((low, high), (low, middle), (middle, high))[0 if half is None else half + 1]

    found = []
    for a, b, step, half in ring_hops(NZ):
        found.append(("z", "z", step, (0, a), (0, b), rows("z", half)))
    for a, b, step, half in ring_hops(NY):
        found.append(("y", "y", step, (a, 0), (b, 0), rows("y", half)))
    for dz in range(NZ):
        for a, b, step, half in ring_hops(NY):
            found.append(("z", "y", step, (a, dz), (b, dz), rows("z", half)))
    for dy in range(NY):
        for a, b, step, half in ring_hops(NZ):
            found.append(("y", "z", step, (dy, a), (dy, b), rows("y", half)))
    return found


def plan(transfers, rate=46e3, latency=2.5):
    have = {("z", 0, 0): [(0, Z_UNITS)], ("y", 0, 0): [(Z_UNITS, PACKED)]}
    waiting = list(range(len(transfers)))
    queues, free, events = {}, {}, []
    arrivals, starts, cause_of = [], {}, {}

    def ready(index):
        part, _, _, (dy, dz), _, (low, high) = transfers[index]
        for a, b in sorted(have.get((part, dy, dz), [])):
            if a <= low < b:
                low = b
        return low >= high

    def pump(now, cause):
        for index in [i for i in waiting if ready(i)]:
            waiting.remove(index)
            queues.setdefault(transfers[index][1:3], []).append(index)
            cause_of[index] = cause
        for link, queue in queues.items():
            if queue and free.get(link, 0.0) <= now:
                queue.sort(key=lambda i: (transfers[i][0] != link[0], i))
                index = queue.pop(0)
                low, high = transfers[index][5]
                took = (high - low) * UNIT * TILE * 2 / rate
                free[link] = now + took
                starts[index] = now
                heapq.heappush(events, (now + took, -1))
                heapq.heappush(events, (now + took + latency, index))

    pump(0.0, -1)
    while events:
        now, index = heapq.heappop(events)
        if index >= 0:
            part, _, _, _, (dy, dz), rows = transfers[index]
            have.setdefault((part, dy, dz), []).append(rows)
            arrivals.append((now, index))
        pump(now, index)
    arrived_at = {index: now for now, index in arrivals}
    released = {-1: []}
    for index in sorted(starts, key=lambda i: (starts[i], i)):
        cause = cause_of[index]
        for now, earlier in arrivals:
            if now > starts[index] - LEAD:
                break
            if cause == -1 or now > arrived_at[cause]:
                cause = earlier
        released.setdefault(cause, []).append(index)
    return arrivals, released


def kernel(
    col_tiles,
    pattern,
    values,
    keep,
    out,
    held,
    last,
    slab,
    dense,
    keep_v,
    pattern_s,
    tiles,
    meta_b,
    meta_a,
    meta_v,
    meta_s,
    tot_y,
    tot_z,
    send_sem,
    recv_sem,
    side_send,
    side_recv,
    small_send,
    small_recv,
    local_sem,
):
    wide, narrow = lax.axis_index("wide"), lax.axis_index("narrow")
    z, y = wide // NY, wide % NY
    x, core = narrow // NC, narrow % NC
    blocks = NX * NC

    def at(dy=0, dz=0):
        return (lax.rem(z + dz, NZ) * NY + lax.rem(y + dy, NY), narrow)

    def beside(dx, dc):
        return (wide, lax.rem(x + dx, NX) * NC + lax.rem(core + dc, NC))

    def remote(src, dst, send, recv, device):
        return pltpu.make_async_remote_copy(
            src_ref=src, dst_ref=dst, send_sem=send, recv_sem=recv, device_id=device, device_id_type=MESH
        )

    pattern_copy = pltpu.make_async_copy(pattern, pattern_s, local_sem.at[2])
    pattern_copy.start()
    tile_copies = []
    for r in range(2):
        for c in range(col_tiles):
            source = values.at[pl.ds(r * TILE, TILE), pl.ds(c * TILE, TILE)]
            p = r * col_tiles + c
            tile_copies.append(pltpu.make_async_copy(source, tiles.at[p], local_sem.at[3 + p]))
            tile_copies[p].start()
    keep_copy = pltpu.make_async_copy(keep, keep_v, local_sem.at[0])
    keep_copy.start()

    z_peers = list(range(1, NZ))
    y_peers = list(range(1, NY))
    x_peers = list(range(1, NX))
    peers = [at(dz=d) for d in z_peers] + [at(dy=d) for d in y_peers] + [beside(d, 0) for d in x_peers]
    sibling = beside(0, 1)
    barrier = pltpu.get_barrier_semaphore()
    for peer in peers:
        pl.semaphore_signal(barrier, inc=1, device_id=peer, device_id_type=MESH)

    @pl.when(core == 0)
    def _():
        pl.semaphore_signal(barrier, inc=1, device_id=sibling, device_id_type=MESH)

    eye = (
        lax.broadcasted_iota(jnp.int32, (TILE, TILE), 0) == lax.broadcasted_iota(jnp.int32, (TILE, TILE), 1)
    ).astype(jnp.float32)
    lane = lax.broadcasted_iota(jnp.int32, (8, TILE), 1)
    def same(a, b):
        return jnp.maximum(0, 1 - jnp.maximum(a - b, b - a))

    zero = jnp.int32(0)
    filled = zero
    picked = [zero] * KEEP
    pattern_copy.wait()
    codes = jnp.zeros((8, TILE), jnp.int32)
    for r in range(2):
        for c in range(col_tiles):
            present = pattern_s[r, c]
            diagonal = jnp.where(2 * wide + r == col_tiles * narrow + c, 1, 0)
            code = present * filled + (1 - present) * (KEEP + diagonal)
            codes = jnp.where(lane == r * col_tiles + c, code, codes)
            for s in range(KEEP):
                mine = present * same(filled, s)
                picked[s] += mine * (r * col_tiles + c)
            filled = filled + present
    shift = 2 * TILE * wide - col_tiles * TILE * narrow
    corner = 2 * wide - col_tiles * narrow
    for copy in tile_copies:
        copy.wait()
    for s, position in enumerate(picked):
        on = same(position, corner) + same(position, corner + 1 + col_tiles)
        inside = jnp.where(jnp.logical_and(corner >= 0, corner < col_tiles), 1, 0)
        on = (on * inside).astype(jnp.float32)
        tile = (tiles[position].astype(jnp.float32) + on * eye).astype(jnp.bfloat16)
        tile = tile.reshape(PART, UNIT, TILE)
        slab[narrow, s * PART : (s + 1) * PART] = tile
        held[0][y, s * PART : (s + 1) * PART] = tile
    meta_b[0, 0] = codes
    meta_a[core, x] = codes

    pl.semaphore_wait(barrier, len(peers) + core)

    transfers = block_transfers()
    arrivals, released = plan(transfers)
    final = transfers[arrivals[-1][1]][4][1]

    def place(dy, dz):
        return last[dy].at[0] if dz == final else held[dz].at[lax.rem(y + dy, NY)]


    def block_copy(index):
        _, axis, step, there, here, (low, high) = transfers[index]
        device = at(dz=step % NZ) if axis == "z" else at(dy=step % NY)
        window = pl.ds(low, high - low)
        if here[1] == final:
            target = last[here[0]].at[0]
        else:
            target = held[here[1]].at[lax.rem(y + there[0], NY)]
        return remote(
            place(*there).at[window], target.at[window], send_sem.at[index], recv_sem.at[index], device
        )

    def block_arrival(index):
        _, axis, step, _, (dy, dz), (low, high) = transfers[index]
        device = at(dz=step % NZ) if axis == "z" else at(dy=step % NY)
        here = place(dy, dz).at[pl.ds(low, high - low)]
        return remote(here, here, send_sem.at[index], recv_sem.at[index], device)

    sent = []

    def start(copy):
        copy.start()
        sent.append(copy)

    for index in released[-1]:
        start(block_copy(index))

    def side_copy(index, block, device):
        ref = slab.at[block, pl.ds(0, PACKED)]
        return remote(ref, ref, side_send.at[index], side_recv.at[index], device)

    own_to_sibling = side_copy(0, narrow, sibling)
    for dx in x_peers:
        start(side_copy(dx, narrow, beside(dx, 0)))
    pl.when(core == 1)(own_to_sibling.start)

    for k, d in enumerate(z_peers):
        start(remote(meta_b.at[0, 0], meta_b.at[0, NZ - d], small_send.at[k], small_recv.at[k], at(dz=d)))
    first_x = len(z_peers)
    for k, dx in enumerate(x_peers):
        k += first_x
        own = meta_a.at[core, x]
        start(remote(own, own, small_send.at[k], small_recv.at[k], beside(dx, 0)))
    first_sibling = first_x + len(x_peers)
    first_y = first_sibling + 1
    first_total = first_y + len(y_peers)

    blank = jnp.zeros((PART, UNIT, TILE), jnp.bfloat16)
    unit = eye.astype(jnp.bfloat16).reshape(PART, UNIT, TILE)
    for ref, count in [(slab, blocks)] + [(held[dz], NY) for dz in range(NZ) if dz != final] + [(ref, 1) for ref in last]:
        for i in range(count):
            ref[i, PACKED : PACKED + PART] = blank
            ref[i, PACKED + PART : PACKED + 2 * PART] = unit

    def meta_along_y():
        for k, d in enumerate(z_peers):
            here = meta_b.at[0, NZ - d]
            remote(here, here, small_send.at[k], small_recv.at[k], at(dz=d)).wait_recv()
        for k, d in enumerate(y_peers):
            k += first_y
            start(remote(meta_b.at[0], meta_b.at[NY - d], small_send.at[k], small_recv.at[k], at(dy=d)))

    def meta_to_scalars():
        theirs = meta_a.at[1 - core]
        remote(theirs, theirs, small_send.at[first_sibling], small_recv.at[first_sibling], sibling).wait_recv()
        for k, d in enumerate(y_peers):
            k += first_y
            here = meta_b.at[NY - d]
            remote(here, here, small_send.at[k], small_recv.at[k], at(dy=d)).wait_recv()
        for dz in range(NZ):
            for dy in range(NY):
                row = dz * NY + dy
                meta_v[row : row + 1, :] = meta_b[dy, dz, 0:1, :]
        for n in range(blocks):
            row = NZ * NY + n
            meta_v[row : row + 1, :] = meta_a[n % NC, n // NC, 0:1, :]
        copy = pltpu.make_async_copy(meta_v, meta_s, local_sem.at[1])
        copy.start()
        copy.wait()

    def side_arrivals():
        @pl.when(core == 0)
        def _():
            side_copy(0, narrow + 1, sibling).wait_recv()
            own_to_sibling.start()

        for k, dx in enumerate(x_peers):
            source = lax.rem(x + NX - dx, NX) * NC + core
            side_copy(dx, source, beside(dx, 0)).wait_recv()
            start(side_copy(NX - 1 + dx, source, sibling))
            k += first_x
            here = meta_a.at[core, lax.rem(x + NX - dx, NX)]
            remote(here, here, small_send.at[k], small_recv.at[k], beside(dx, 0)).wait_recv()
        ours = meta_a.at[core]
        start(remote(ours, ours, small_send.at[first_sibling], small_recv.at[first_sibling], sibling))
        sent.append(own_to_sibling)

    def tile_of(ref, block, code):
        return ref[block, pl.ds(code * PART, PART)].reshape(TILE, TILE)

    def expand_slab():
        @pl.when(core == 1)
        def _():
            side_copy(0, narrow - 1, sibling).wait_recv()

        for dx in x_peers:
            source = lax.rem(x + NX - dx, NX) * NC + 1 - core
            side_copy(NX - 1 + dx, source, sibling).wait_recv()

        def body(n, carry):
            for r in range(2):
                for c in range(col_tiles):
                    code = meta_s[NZ * NY + n, r * col_tiles + c]
                    dense[n, r * TILE : (r + 1) * TILE, c * TILE : (c + 1) * TILE] = tile_of(slab, n, code)
            return carry

        lax.fori_loop(0, blocks, body, 0)

    row_id = lax.broadcasted_iota(jnp.int32, (2 * TILE, TILE), 0)
    col_id = lax.broadcasted_iota(jnp.int32, (2 * TILE, TILE), 1)

    def strip(ref, row, dy, dz, pair):
        halves = []
        for r in range(2):
            codes = [meta_s[dz * NY + dy, r * col_tiles + pair * 2 + c] for c in range(2)]
            halves.append(jnp.concatenate([tile_of(ref, row, code) for code in codes], axis=1))
        return halves

    def multiply_plane(dz, pair, first):
        halves = []
        for row in range(NY):
            halves += strip(held[dz], row, lax.rem(row - y + NY, NY), dz, pair)
        product = jnp.dot(
            dense[lax.rem(z + dz, NZ)], jnp.concatenate(halves, axis=0), preferred_element_type=jnp.float32
        )
        columns = slice(pair * 2 * TILE, (pair + 1) * 2 * TILE)
        if first:
            out[:, columns] = product
        else:
            out[:, columns] += product

    def multiply_block(dy, pair, finish):
        depth = pl.ds(pl.multiple_of(lax.rem(y + dy, NY) * 2 * TILE, 2 * TILE), 2 * TILE)
        rhs = jnp.concatenate(strip(last[dy], 0, dy, final, pair), axis=0)
        product = jnp.dot(dense[lax.rem(z + final, NZ), :, depth], rhs, preferred_element_type=jnp.float32)
        columns = slice(pair * 2 * TILE, (pair + 1) * 2 * TILE)
        if not finish:
            out[:, columns] += product
            return
        product = out[:, columns] + product
        for half in range(2):
            c = pair * 2 + half
            columns = slice(c * TILE, (c + 1) * TILE)
            value = product[:, half * TILE : (half + 1) * TILE]
            kept = jnp.logical_or(keep_v[:, columns] == 1, row_id + shift == col_id + c * TILE)
            pruned = jnp.where(kept, value * value, 0.0)
            out[:, columns] = pruned
            tot_y[0, c : c + 1, :] = jnp.sum(pruned, axis=0, keepdims=True)

    extras = [(8.0, meta_along_y), (10.0, side_arrivals), (14.0, meta_to_scalars), (15.0, expand_slab)]
    pairs = col_tiles // 2
    left = {}

    def unit_of(index):
        dy, dz = transfers[index][4]
        return (dy, dz) if dz == final else (None, dz)

    for _, index in arrivals:
        left[unit_of(index)] = left.get(unit_of(index), 0) + 1
    blocks_left = NY
    queue, multiplied = [], []
    issued, settled = [], 0
    clock = 0.0

    def run(budget):
        nonlocal clock
        while queue and extras == [] and clock + queue[0][0] <= budget:
            cost, action = queue.pop(0)
            action()
            clock += cost

    for now, index in arrivals:
        end = index == arrivals[-1][1]
        while extras and (end or extras[0][0] <= now):
            extras.pop(0)[1]()
        run(float("inf") if end else now)
        block_arrival(index).wait_recv()
        clock = max(clock, now)
        for following in released.get(index, []):
            start(block_copy(following))
        issued.append(len(sent))
        while len(issued) > RETIRE and settled < issued[-RETIRE]:
            sent[settled].wait_send()
            settled += 1
        left[unit_of(index)] -= 1
        if left[unit_of(index)] == 0:
            dy, dz = unit_of(index)
            for pair in range(pairs):
                if dy is None:
                    queue.append((0.3, functools.partial(multiply_plane, dz, pair, not multiplied)))
                else:
                    queue.append((0.1, functools.partial(multiply_block, dy, pair, blocks_left == 1)))
            if dy is None:
                multiplied.append(dz)
            else:
                blocks_left -= 1
    keep_copy.wait()
    if col_tiles < 8:
        tot_y[0] = jnp.ones((8, TILE), jnp.float32)
    run(float("inf"))

    for k, d in enumerate(y_peers):
        k += first_total
        start(remote(tot_y.at[0], tot_y.at[NY - d], small_send.at[k], small_recv.at[k], at(dy=d)))
    before = len(sent) - len(y_peers)
    for copy in sent[settled:before]:
        copy.wait_send()
    for k, d in enumerate(y_peers):
        k += first_total
        here = tot_y.at[NY - d]
        remote(here, here, small_send.at[k], small_recv.at[k], at(dy=d)).wait_recv()
    tot_z[0] = functools.reduce(jnp.add, [tot_y[d] for d in range(NY)])
    first_total_z = first_total + len(y_peers)
    for k, d in enumerate(z_peers):
        k += first_total_z
        start(remote(tot_z.at[0], tot_z.at[NZ - d], small_send.at[k], small_recv.at[k], at(dz=d)))
    for k, d in enumerate(z_peers):
        k += first_total_z
        here = tot_z.at[NZ - d]
        remote(here, here, small_send.at[k], small_recv.at[k], at(dz=d)).wait_recv()
    total = functools.reduce(jnp.add, [tot_z[d] for d in range(NZ)])
    scale = (2 * TILE * NZ * NY) / total
    for c in range(col_tiles):
        columns = slice(c * TILE, (c + 1) * TILE)
        out[:, columns] = out[:, columns] * scale[c : c + 1, :]
    for copy in sent[before:]:
        copy.wait_send()


def shards(values, pattern, keep_mask):
    rows, cols = values.shape
    col_tiles = cols // TILE
    blocks = NX * NC
    transfers = len(block_transfers())
    small = 2 * (NZ - 1) + 2 * (NY - 1) + NX
    return pl.pallas_call(
        functools.partial(kernel, col_tiles),
        out_shape=jax.ShapeDtypeStruct((rows, cols), jnp.float32),
        in_specs=[
            pl.BlockSpec(memory_space=pltpu.HBM),
            pl.BlockSpec(memory_space=pltpu.HBM),
            pl.BlockSpec(memory_space=pltpu.HBM),
        ],
        out_specs=pl.BlockSpec(memory_space=pltpu.VMEM),
        scratch_shapes=[
            [pltpu.VMEM((NY, SLOTS * PART, UNIT, TILE), jnp.bfloat16) for _ in range(NZ)],
            [pltpu.VMEM((1, SLOTS * PART, UNIT, TILE), jnp.bfloat16) for _ in range(NY)],
            pltpu.VMEM((blocks, SLOTS * PART, UNIT, TILE), jnp.bfloat16),
            pltpu.VMEM((blocks, rows, cols), jnp.bfloat16),
            pltpu.VMEM((rows, cols), jnp.int32),
            pltpu.SMEM((2, col_tiles), jnp.int32),
            pltpu.VMEM((2 * col_tiles, TILE, TILE), jnp.bfloat16),
            pltpu.VMEM((NY, NZ, 8, TILE), jnp.int32),
            pltpu.VMEM((NC, NX, 8, TILE), jnp.int32),
            pltpu.VMEM((NZ * NY + blocks, TILE), jnp.int32),
            pltpu.SMEM((NZ * NY + blocks, TILE), jnp.int32),
            pltpu.VMEM((NY, 8, TILE), jnp.float32),
            pltpu.VMEM((NZ, 8, TILE), jnp.float32),
            pltpu.SemaphoreType.DMA((transfers,)),
            pltpu.SemaphoreType.DMA((transfers,)),
            pltpu.SemaphoreType.DMA((2 * NX - 1,)),
            pltpu.SemaphoreType.DMA((2 * NX - 1,)),
            pltpu.SemaphoreType.DMA((small,)),
            pltpu.SemaphoreType.DMA((small,)),
            pltpu.SemaphoreType.DMA((3 + 2 * col_tiles,)),
        ],
        compiler_params=pltpu.CompilerParams(
            collective_id=0, has_side_effects=True, vmem_limit_bytes=52 * 1024 * 1024
        ),
        cost_estimate=pl.CostEstimate(flops=2 * rows * cols * 8192, bytes_accessed=12 << 20, transcendentals=0),
    )(*[pltpu.with_memory_space_constraint(operand, pltpu.HBM) for operand in (pattern, values, keep_mask)])


def solution(mesh):
    return jax.shard_map(
        shards,
        mesh=mesh,
        in_specs=(P("wide", "narrow"), P("wide", "narrow"), P("wide", "narrow")),
        out_specs=P("wide", "narrow"),
        check_vma=False,
    )
```

```python
import functools
import heapq

import jax
import jax.numpy as jnp
from jax import lax
from jax.experimental import pallas as pl
from jax.experimental.pallas import tpu as pltpu
from jax.sharding import PartitionSpec as P

TILE = 128
KEEP = 6
SLOTS = KEEP + 2
UNIT = 32
PART = TILE // UNIT
PACKED = KEEP * PART
NZ, NY, NX, NC = 8, 4, 4, 2
RETIRE = 20
LEADS = (0.5, 2.5)
Z_UNITS = 14
MESH = pl.DeviceIdType.MESH


def ring_hops(n):
    full = (n - 1) // 2
    hops = []
    for step in (1, -1):
        for hop in range(full):
            hops.append(((-step * hop) % n, (-step * (hop + 1)) % n, step, None))
        if n % 2 == 0:
            half = 0 if step == 1 else 1
            hops.append(((-step * full) % n, (-step * (full + 1)) % n, step, half))
    return hops


def block_transfers():
    def rows(part, half):
        low, high = (0, Z_UNITS) if part == "z" else (Z_UNITS, PACKED)
        middle = (low + high) // 2
        return ((low, high), (low, middle), (middle, high))[0 if half is None else half + 1]

    found = []
    for a, b, step, half in ring_hops(NZ):
        found.append(("z", "z", step, (0, a), (0, b), rows("z", half)))
    for a, b, step, half in ring_hops(NY):
        found.append(("y", "y", step, (a, 0), (b, 0), rows("y", half)))
    for dz in range(NZ):
        for a, b, step, half in ring_hops(NY):
            found.append(("z", "y", step, (a, dz), (b, dz), rows("z", half)))
    for dy in range(NY):
        for a, b, step, half in ring_hops(NZ):
            found.append(("y", "z", step, (dy, a), (dy, b), rows("y", half)))
    return found


def plan(transfers, lead, rate=60e3, latency=2.5):
    have = {("z", 0, 0): [(0, Z_UNITS)], ("y", 0, 0): [(Z_UNITS, PACKED)]}
    waiting = list(range(len(transfers)))
    queues, free, events = {}, {}, []
    arrivals, starts, cause_of = [], {}, {}

    def ready(index):
        part, _, _, (dy, dz), _, (low, high) = transfers[index]
        for a, b in sorted(have.get((part, dy, dz), [])):
            if a <= low < b:
                low = b
        return low >= high

    def pump(now, cause):
        for index in [i for i in waiting if ready(i)]:
            waiting.remove(index)
            queues.setdefault(transfers[index][1:3], []).append(index)
            cause_of[index] = cause
        for link, queue in queues.items():
            if queue and free.get(link, 0.0) <= now:
                queue.sort(key=lambda i: (transfers[i][0] != link[0], i))
                index = queue.pop(0)
                low, high = transfers[index][5]
                took = (high - low) * UNIT * TILE * 2 / rate
                free[link] = now + took
                starts[index] = now
                heapq.heappush(events, (now + took, -1))
                heapq.heappush(events, (now + took + latency, index))

    pump(0.0, -1)
    while events:
        now, index = heapq.heappop(events)
        if index >= 0:
            part, _, _, _, (dy, dz), rows = transfers[index]
            have.setdefault((part, dy, dz), []).append(rows)
            arrivals.append((now, index))
        pump(now, index)
    arrived_at = {index: now for now, index in arrivals}
    released = {-1: []}
    for index in sorted(starts, key=lambda i: (starts[i], i)):
        cause = cause_of[index]
        for now, earlier in arrivals:
            if now > starts[index] - lead:
                break
            if cause == -1 or now > arrived_at[cause]:
                cause = earlier
        released.setdefault(cause, []).append(index)
    return arrivals, released


def kernel(
    col_tiles,
    pattern,
    values,
    keep,
    out,
    held,
    last,
    slab,
    dense,
    keep_v,
    pattern_s,
    values_v,
    tiles,
    meta_b,
    meta_a,
    meta_v,
    meta_s,
    tot_y,
    tot_z,
    send_sem,
    recv_sem,
    side_send,
    side_recv,
    small_send,
    small_recv,
    local_sem,
):
    wide, narrow = lax.axis_index("wide"), lax.axis_index("narrow")
    z, y = wide // NY, wide % NY
    x, core = narrow // NC, narrow % NC
    blocks = NX * NC

    def at(dy=0, dz=0):
        return (lax.rem(z + dz, NZ) * NY + lax.rem(y + dy, NY), narrow)

    def beside(dx, dc):
        return (wide, lax.rem(x + dx, NX) * NC + lax.rem(core + dc, NC))

    def remote(src, dst, send, recv, device):
        return pltpu.make_async_remote_copy(
            src_ref=src, dst_ref=dst, send_sem=send, recv_sem=recv, device_id=device, device_id_type=MESH
        )

    pattern_copy = pltpu.make_async_copy(pattern, pattern_s, local_sem.at[1])
    pattern_copy.start()
    values_copy = pltpu.make_async_copy(values, values_v, local_sem.at[2])
    values_copy.start()
    z_peers = list(range(1, NZ))
    y_peers = list(range(1, NY))
    x_peers = list(range(1, NX))
    peers = [at(dz=d) for d in z_peers] + [at(dy=d) for d in y_peers] + [beside(d, 0) for d in x_peers]
    sibling = beside(0, 1)
    barrier = pltpu.get_barrier_semaphore()
    for peer in peers:
        pl.semaphore_signal(barrier, inc=1, device_id=peer, device_id_type=MESH)

    @pl.when(core == 0)
    def _():
        pl.semaphore_signal(barrier, inc=1, device_id=sibling, device_id_type=MESH)

    eye = (
        lax.broadcasted_iota(jnp.int32, (TILE, TILE), 0) == lax.broadcasted_iota(jnp.int32, (TILE, TILE), 1)
    ).astype(jnp.float32)
    lane = lax.broadcasted_iota(jnp.int32, (8, TILE), 1)
    def same(a, b):
        return jnp.maximum(0, 1 - jnp.maximum(a - b, b - a))

    zero = jnp.int32(0)
    filled = zero
    picked = [zero] * KEEP
    pattern_copy.wait()
    codes = jnp.zeros((8, TILE), jnp.int32)
    for r in range(2):
        for c in range(col_tiles):
            present = pattern_s[r, c]
            diagonal = jnp.where(2 * wide + r == col_tiles * narrow + c, 1, 0)
            code = present * filled + (1 - present) * (KEEP + diagonal)
            codes = jnp.where(lane == r * col_tiles + c, code, codes)
            for s in range(KEEP):
                mine = present * same(filled, s)
                picked[s] += mine * (r * col_tiles + c)
            filled = filled + present
    shift = 2 * TILE * wide - col_tiles * TILE * narrow
    corner = 2 * wide - col_tiles * narrow
    values_copy.wait()
    for r in range(2):
        for c in range(col_tiles):
            tiles[r * col_tiles + c] = values_v[r * TILE : (r + 1) * TILE, c * TILE : (c + 1) * TILE]
    for s, position in enumerate(picked):
        on = same(position, corner) + same(position, corner + 1 + col_tiles)
        inside = jnp.where(jnp.logical_and(corner >= 0, corner < col_tiles), 1, 0)
        on = (on * inside).astype(jnp.float32)
        tile = (tiles[position].astype(jnp.float32) + on * eye).astype(jnp.bfloat16)
        tile = tile.reshape(PART, UNIT, TILE)
        slab[narrow, s * PART : (s + 1) * PART] = tile
        held[0][y, s * PART : (s + 1) * PART] = tile
    meta_b[0, 0] = codes
    meta_a[core, x] = codes

    pl.semaphore_wait(barrier, len(peers) + core)

    transfers = block_transfers()
    arrivals, _ = plan(transfers, LEADS[0])
    released = [plan(transfers, lead)[1] for lead in LEADS]
    final = transfers[arrivals[-1][1]][4][1]

    def place(dy, dz):
        return last[dy].at[0] if dz == final else held[dz].at[lax.rem(y + dy, NY)]


    def block_copy(index):
        _, axis, step, there, here, (low, high) = transfers[index]
        device = at(dz=step % NZ) if axis == "z" else at(dy=step % NY)
        window = pl.ds(low, high - low)
        if here[1] == final:
            target = last[here[0]].at[0]
        else:
            target = held[here[1]].at[lax.rem(y + there[0], NY)]
        return remote(
            place(*there).at[window], target.at[window], send_sem.at[index], recv_sem.at[index], device
        )

    def block_arrival(index):
        _, axis, step, _, (dy, dz), (low, high) = transfers[index]
        device = at(dz=step % NZ) if axis == "z" else at(dy=step % NY)
        here = place(dy, dz).at[pl.ds(low, high - low)]
        return remote(here, here, send_sem.at[index], recv_sem.at[index], device)

    sent = []

    def start(copy):
        copy.start()
        sent.append(copy)

    half_started = set()

    def start_after(event):
        first, second = (plan_.get(event, []) for plan_ in released)
        for index in first:
            if index in second:
                start(block_copy(index))
        for which, some, others in ((0, first, second), (1, second, first)):
            for index in some:
                if index in others:
                    continue
                copy = block_copy(index)
                pl.when(core == which)(copy.start)
                if index in half_started:
                    sent.append(copy)
                half_started.add(index)

    start_after(-1)

    def side_copy(index, block, device):
        ref = slab.at[block, pl.ds(0, PACKED)]
        return remote(ref, ref, side_send.at[index], side_recv.at[index], device)

    own_to_sibling = side_copy(0, narrow, sibling)
    for dx in x_peers:
        start(side_copy(dx, narrow, beside(dx, 0)))
    pl.when(core == 1)(own_to_sibling.start)

    for k, d in enumerate(z_peers):
        start(remote(meta_b.at[0, 0], meta_b.at[0, NZ - d], small_send.at[k], small_recv.at[k], at(dz=d)))
    first_x = len(z_peers)
    for k, dx in enumerate(x_peers):
        k += first_x
        own = meta_a.at[core, x]
        start(remote(own, own, small_send.at[k], small_recv.at[k], beside(dx, 0)))
    first_sibling = first_x + len(x_peers)
    first_y = first_sibling + 1
    first_total = first_y + len(y_peers)

    keep_copy = pltpu.make_async_copy(keep, keep_v, local_sem.at[0])
    keep_copy.start()
    blank = jnp.zeros((PART, UNIT, TILE), jnp.bfloat16)
    unit = eye.astype(jnp.bfloat16).reshape(PART, UNIT, TILE)
    for ref, count in [(slab, blocks)] + [(held[dz], NY) for dz in range(NZ) if dz != final] + [(ref, 1) for ref in last]:
        for i in range(count):
            ref[i, PACKED : PACKED + PART] = blank
            ref[i, PACKED + PART : PACKED + 2 * PART] = unit

    def meta_along_y():
        for k, d in enumerate(z_peers):
            here = meta_b.at[0, NZ - d]
            remote(here, here, small_send.at[k], small_recv.at[k], at(dz=d)).wait_recv()
        for k, d in enumerate(y_peers):
            k += first_y
            start(remote(meta_b.at[0], meta_b.at[NY - d], small_send.at[k], small_recv.at[k], at(dy=d)))

    def meta_to_scalars():
        theirs = meta_a.at[1 - core]
        remote(theirs, theirs, small_send.at[first_sibling], small_recv.at[first_sibling], sibling).wait_recv()
        for k, d in enumerate(y_peers):
            k += first_y
            here = meta_b.at[NY - d]
            remote(here, here, small_send.at[k], small_recv.at[k], at(dy=d)).wait_recv()
        for dz in range(NZ):
            for dy in range(NY):
                row = dz * NY + dy
                meta_v[row : row + 1, :] = meta_b[dy, dz, 0:1, :]
        for n in range(blocks):
            row = NZ * NY + n
            meta_v[row : row + 1, :] = meta_a[n % NC, n // NC, 0:1, :]
        copy = pltpu.make_async_copy(meta_v, meta_s, local_sem.at[3])
        copy.start()
        copy.wait()

    def side_arrivals():
        @pl.when(core == 0)
        def _():
            side_copy(0, narrow + 1, sibling).wait_recv()
            own_to_sibling.start()

        for k, dx in enumerate(x_peers):
            source = lax.rem(x + NX - dx, NX) * NC + core
            side_copy(dx, source, beside(dx, 0)).wait_recv()
            start(side_copy(NX - 1 + dx, source, sibling))
            k += first_x
            here = meta_a.at[core, lax.rem(x + NX - dx, NX)]
            remote(here, here, small_send.at[k], small_recv.at[k], beside(dx, 0)).wait_recv()
        ours = meta_a.at[core]
        start(remote(ours, ours, small_send.at[first_sibling], small_recv.at[first_sibling], sibling))
        sent.append(own_to_sibling)

    def tile_of(ref, block, code):
        return ref[block, pl.ds(code * PART, PART)].reshape(TILE, TILE)

    def expand_slab():
        @pl.when(core == 1)
        def _():
            side_copy(0, narrow - 1, sibling).wait_recv()

        for dx in x_peers:
            source = lax.rem(x + NX - dx, NX) * NC + 1 - core
            side_copy(NX - 1 + dx, source, sibling).wait_recv()

        def body(n, carry):
            for r in range(2):
                for c in range(col_tiles):
                    code = meta_s[NZ * NY + n, r * col_tiles + c]
                    dense[n, r * TILE : (r + 1) * TILE, c * TILE : (c + 1) * TILE] = tile_of(slab, n, code)
            return carry

        lax.fori_loop(0, blocks, body, 0)

    row_id = lax.broadcasted_iota(jnp.int32, (2 * TILE, TILE), 0)
    col_id = lax.broadcasted_iota(jnp.int32, (2 * TILE, TILE), 1)

    def strip(ref, row, dy, dz, pair):
        halves = []
        for r in range(2):
            codes = [meta_s[dz * NY + dy, r * col_tiles + pair * 2 + c] for c in range(2)]
            halves.append(jnp.concatenate([tile_of(ref, row, code) for code in codes], axis=1))
        return halves

    def multiply_plane(dz, pair, first):
        halves = []
        for row in range(NY):
            halves += strip(held[dz], row, lax.rem(row - y + NY, NY), dz, pair)
        product = jnp.dot(
            dense[lax.rem(z + dz, NZ)], jnp.concatenate(halves, axis=0), preferred_element_type=jnp.float32
        )
        columns = slice(pair * 2 * TILE, (pair + 1) * 2 * TILE)
        if first:
            out[:, columns] = product
        else:
            out[:, columns] += product

    def multiply_block(dy, pair, finish):
        depth = pl.ds(pl.multiple_of(lax.rem(y + dy, NY) * 2 * TILE, 2 * TILE), 2 * TILE)
        rhs = jnp.concatenate(strip(last[dy], 0, dy, final, pair), axis=0)
        product = jnp.dot(dense[lax.rem(z + final, NZ), :, depth], rhs, preferred_element_type=jnp.float32)
        columns = slice(pair * 2 * TILE, (pair + 1) * 2 * TILE)
        if not finish:
            out[:, columns] += product
            return
        product = out[:, columns] + product
        for half in range(2):
            c = pair * 2 + half
            columns = slice(c * TILE, (c + 1) * TILE)
            value = product[:, half * TILE : (half + 1) * TILE]
            kept = jnp.logical_or(keep_v[:, columns] == 1, row_id + shift == col_id + c * TILE)
            pruned = jnp.where(kept, value * value, 0.0)
            out[:, columns] = pruned
            tot_y[0, c : c + 1, :] = jnp.sum(pruned, axis=0, keepdims=True)

    extras = [(9.0, meta_along_y), (17.0, side_arrivals), (18.0, meta_to_scalars), (21.0, expand_slab)]
    pairs = col_tiles // 2
    left = {}

    def unit_of(index):
        dy, dz = transfers[index][4]
        return (dy, dz) if dz == final else (None, dz)

    for _, index in arrivals:
        left[unit_of(index)] = left.get(unit_of(index), 0) + 1
    blocks_left = NY
    queue, multiplied = [], []
    issued, settled = [], 0
    clock = 0.0

    def run(budget):
        nonlocal clock
        while queue and extras == [] and clock + queue[0][0] <= budget:
            cost, action = queue.pop(0)
            action()
            clock += cost

    for now, index in arrivals:
        end = index == arrivals[-1][1]
        while extras and (end or extras[0][0] <= now):
            extras.pop(0)[1]()
        run(float("inf") if end else now)
        block_arrival(index).wait_recv()
        clock = max(clock, now)
        start_after(index)
        issued.append(len(sent))
        while len(issued) > RETIRE and settled < issued[-RETIRE]:
            sent[settled].wait_send()
            settled += 1
        left[unit_of(index)] -= 1
        if left[unit_of(index)] == 0:
            dy, dz = unit_of(index)
            for pair in range(pairs):
                if dy is None:
                    queue.append((0.3, functools.partial(multiply_plane, dz, pair, not multiplied)))
                else:
                    queue.append((0.1, functools.partial(multiply_block, dy, pair, blocks_left == 1)))
            if dy is None:
                multiplied.append(dz)
            else:
                blocks_left -= 1
    keep_copy.wait()
    if col_tiles < 8:
        tot_y[0] = jnp.ones((8, TILE), jnp.float32)
    run(float("inf"))

    for k, d in enumerate(y_peers):
        k += first_total
        start(remote(tot_y.at[0], tot_y.at[NY - d], small_send.at[k], small_recv.at[k], at(dy=d)))
    before = len(sent) - len(y_peers)
    for copy in sent[settled:before]:
        copy.wait_send()
    for k, d in enumerate(y_peers):
        k += first_total
        here = tot_y.at[NY - d]
        remote(here, here, small_send.at[k], small_recv.at[k], at(dy=d)).wait_recv()
    tot_z[0] = functools.reduce(jnp.add, [tot_y[d] for d in range(NY)])
    first_total_z = first_total + len(y_peers)
    for k, d in enumerate(z_peers):
        k += first_total_z
        start(remote(tot_z.at[0], tot_z.at[NZ - d], small_send.at[k], small_recv.at[k], at(dz=d)))
    for k, d in enumerate(z_peers):
        k += first_total_z
        here = tot_z.at[NZ - d]
        remote(here, here, small_send.at[k], small_recv.at[k], at(dz=d)).wait_recv()
    total = functools.reduce(jnp.add, [tot_z[d] for d in range(NZ)])
    scale = (2 * TILE * NZ * NY) / total
    for c in range(col_tiles):
        columns = slice(c * TILE, (c + 1) * TILE)
        out[:, columns] = out[:, columns] * scale[c : c + 1, :]
    for copy in sent[before:]:
        copy.wait_send()


def shards(values, pattern, keep_mask):
    rows, cols = values.shape
    col_tiles = cols // TILE
    blocks = NX * NC
    transfers = len(block_transfers())
    small = 2 * (NZ - 1) + 2 * (NY - 1) + NX
    return pl.pallas_call(
        functools.partial(kernel, col_tiles),
        out_shape=jax.ShapeDtypeStruct((rows, cols), jnp.float32),
        in_specs=[
            pl.BlockSpec(memory_space=pltpu.HBM),
            pl.BlockSpec(memory_space=pltpu.HBM),
            pl.BlockSpec(memory_space=pltpu.HBM),
        ],
        out_specs=pl.BlockSpec(memory_space=pltpu.VMEM),
        scratch_shapes=[
            [pltpu.VMEM((NY, SLOTS * PART, UNIT, TILE), jnp.bfloat16) for _ in range(NZ)],
            [pltpu.VMEM((1, SLOTS * PART, UNIT, TILE), jnp.bfloat16) for _ in range(NY)],
            pltpu.VMEM((blocks, SLOTS * PART, UNIT, TILE), jnp.bfloat16),
            pltpu.VMEM((blocks, rows, cols), jnp.bfloat16),
            pltpu.VMEM((rows, cols), jnp.int32),
            pltpu.SMEM((2, col_tiles), jnp.int32),
            pltpu.VMEM((rows, cols), jnp.bfloat16),
            pltpu.VMEM((2 * col_tiles, TILE, TILE), jnp.bfloat16),
            pltpu.VMEM((NY, NZ, 8, TILE), jnp.int32),
            pltpu.VMEM((NC, NX, 8, TILE), jnp.int32),
            pltpu.VMEM((NZ * NY + blocks, TILE), jnp.int32),
            pltpu.SMEM((NZ * NY + blocks, TILE), jnp.int32),
            pltpu.VMEM((NY, 8, TILE), jnp.float32),
            pltpu.VMEM((NZ, 8, TILE), jnp.float32),
            pltpu.SemaphoreType.DMA((transfers,)),
            pltpu.SemaphoreType.DMA((transfers,)),
            pltpu.SemaphoreType.DMA((2 * NX - 1,)),
            pltpu.SemaphoreType.DMA((2 * NX - 1,)),
            pltpu.SemaphoreType.DMA((small,)),
            pltpu.SemaphoreType.DMA((small,)),
            pltpu.SemaphoreType.DMA((4,)),
        ],
        compiler_params=pltpu.CompilerParams(
            collective_id=0, has_side_effects=True, vmem_limit_bytes=52 * 1024 * 1024
        ),
        cost_estimate=pl.CostEstimate(flops=2 * rows * cols * 8192, bytes_accessed=12 << 20, transcendentals=0),
    )(*[pltpu.with_memory_space_constraint(operand, pltpu.HBM) for operand in (pattern, values, keep_mask)])


def solution(mesh):
    return jax.shard_map(
        shards,
        mesh=mesh,
        in_specs=(P("wide", "narrow"), P("wide", "narrow"), P("wide", "narrow")),
        out_specs=P("wide", "narrow"),
        check_vma=False,
    )
```

```python
import functools
import heapq

import jax
import jax.numpy as jnp
from jax import lax
from jax.experimental import pallas as pl
from jax.experimental.pallas import tpu as pltpu
from jax.sharding import PartitionSpec as P

TILE = 128
KEEP = 6
SLOTS = KEEP + 2
UNIT = 32
PART = TILE // UNIT
PACKED = KEEP * PART
NZ, NY, NX, NC = 8, 4, 4, 2
RETIRE = 20
LEADS = (0.5, 2.5)
Z_UNITS = 14
MESH = pl.DeviceIdType.MESH


def ring_hops(n):
    full = (n - 1) // 2
    hops = []
    for step in (1, -1):
        for hop in range(full):
            hops.append(((-step * hop) % n, (-step * (hop + 1)) % n, step, None))
        if n % 2 == 0:
            half = 0 if step == 1 else 1
            hops.append(((-step * full) % n, (-step * (full + 1)) % n, step, half))
    return hops


def block_transfers():
    def rows(part, half):
        low, high = (0, Z_UNITS) if part == "z" else (Z_UNITS, PACKED)
        middle = (low + high) // 2
        return ((low, high), (low, middle), (middle, high))[0 if half is None else half + 1]

    found = []
    for a, b, step, half in ring_hops(NZ):
        found.append(("z", "z", step, (0, a), (0, b), rows("z", half)))
    for a, b, step, half in ring_hops(NY):
        found.append(("y", "y", step, (a, 0), (b, 0), rows("y", half)))
    for dz in range(NZ):
        for a, b, step, half in ring_hops(NY):
            found.append(("z", "y", step, (a, dz), (b, dz), rows("z", half)))
    for dy in range(NY):
        for a, b, step, half in ring_hops(NZ):
            found.append(("y", "z", step, (dy, a), (dy, b), rows("y", half)))
    return found


def plan(transfers, lead, rate=60e3, latency=3.0):
    have = {("z", 0, 0): [(0, Z_UNITS)], ("y", 0, 0): [(Z_UNITS, PACKED)]}
    waiting = list(range(len(transfers)))
    queues, free, events = {}, {}, []
    arrivals, starts, cause_of = [], {}, {}

    def ready(index):
        part, _, _, (dy, dz), _, (low, high) = transfers[index]
        for a, b in sorted(have.get((part, dy, dz), [])):
            if a <= low < b:
                low = b
        return low >= high

    def pump(now, cause):
        for index in [i for i in waiting if ready(i)]:
            waiting.remove(index)
            queues.setdefault(transfers[index][1:3], []).append(index)
            cause_of[index] = cause
        for link, queue in queues.items():
            if queue and free.get(link, 0.0) <= now:
                queue.sort(key=lambda i: (transfers[i][0] != link[0], i))
                index = queue.pop(0)
                low, high = transfers[index][5]
                took = (high - low) * UNIT * TILE * 2 / rate
                free[link] = now + took
                starts[index] = now
                heapq.heappush(events, (now + took, -1))
                heapq.heappush(events, (now + took + latency, index))

    pump(0.0, -1)
    while events:
        now, index = heapq.heappop(events)
        if index >= 0:
            part, _, _, _, (dy, dz), rows = transfers[index]
            have.setdefault((part, dy, dz), []).append(rows)
            arrivals.append((now, index))
        pump(now, index)
    arrived_at = {index: now for now, index in arrivals}
    released = {-1: []}
    for index in sorted(starts, key=lambda i: (starts[i], i)):
        cause = cause_of[index]
        for now, earlier in arrivals:
            if now > starts[index] - lead:
                break
            if cause == -1 or now > arrived_at[cause]:
                cause = earlier
        released.setdefault(cause, []).append(index)
    return arrivals, released


def kernel(
    col_tiles,
    pattern,
    values,
    keep,
    out,
    held,
    last,
    slab,
    dense,
    keep_v,
    pattern_s,
    values_v,
    tiles,
    meta_b,
    meta_a,
    meta_v,
    meta_s,
    tot_y,
    tot_z,
    send_sem,
    recv_sem,
    side_send,
    side_recv,
    small_send,
    small_recv,
    local_sem,
):
    wide, narrow = lax.axis_index("wide"), lax.axis_index("narrow")
    z, y = wide // NY, wide % NY
    x, core = narrow // NC, narrow % NC
    blocks = NX * NC

    def at(dy=0, dz=0):
        return (lax.rem(z + dz, NZ) * NY + lax.rem(y + dy, NY), narrow)

    def beside(dx, dc):
        return (wide, lax.rem(x + dx, NX) * NC + lax.rem(core + dc, NC))

    def remote(src, dst, send, recv, device):
        return pltpu.make_async_remote_copy(
            src_ref=src, dst_ref=dst, send_sem=send, recv_sem=recv, device_id=device, device_id_type=MESH
        )

    pattern_copy = pltpu.make_async_copy(pattern, pattern_s, local_sem.at[1])
    pattern_copy.start()
    values_copy = pltpu.make_async_copy(values, values_v, local_sem.at[2])
    values_copy.start()
    z_peers = list(range(1, NZ))
    y_peers = list(range(1, NY))
    x_peers = list(range(1, NX))
    peers = [at(dz=d) for d in z_peers] + [at(dy=d) for d in y_peers] + [beside(d, 0) for d in x_peers]
    sibling = beside(0, 1)
    barrier = pltpu.get_barrier_semaphore()
    for peer in peers:
        pl.semaphore_signal(barrier, inc=1, device_id=peer, device_id_type=MESH)

    @pl.when(core == 0)
    def _():
        pl.semaphore_signal(barrier, inc=1, device_id=sibling, device_id_type=MESH)

    eye = (
        lax.broadcasted_iota(jnp.int32, (TILE, TILE), 0) == lax.broadcasted_iota(jnp.int32, (TILE, TILE), 1)
    ).astype(jnp.float32)
    lane = lax.broadcasted_iota(jnp.int32, (8, TILE), 1)
    def same(a, b):
        return jnp.maximum(0, 1 - jnp.maximum(a - b, b - a))

    zero = jnp.int32(0)
    filled = zero
    picked = [zero] * KEEP
    pattern_copy.wait()
    codes = jnp.zeros((8, TILE), jnp.int32)
    for r in range(2):
        for c in range(col_tiles):
            present = pattern_s[r, c]
            diagonal = jnp.where(2 * wide + r == col_tiles * narrow + c, 1, 0)
            code = present * filled + (1 - present) * (KEEP + diagonal)
            codes = jnp.where(lane == r * col_tiles + c, code, codes)
            for s in range(KEEP):
                mine = present * same(filled, s)
                picked[s] += mine * (r * col_tiles + c)
            filled = filled + present
    shift = 2 * TILE * wide - col_tiles * TILE * narrow
    corner = 2 * wide - col_tiles * narrow
    values_copy.wait()
    for r in range(2):
        for c in range(col_tiles):
            tiles[r * col_tiles + c] = values_v[r * TILE : (r + 1) * TILE, c * TILE : (c + 1) * TILE]
    for s, position in enumerate(picked):
        on = same(position, corner) + same(position, corner + 1 + col_tiles)
        inside = jnp.where(jnp.logical_and(corner >= 0, corner < col_tiles), 1, 0)
        on = (on * inside).astype(jnp.float32)
        tile = (tiles[position].astype(jnp.float32) + on * eye).astype(jnp.bfloat16)
        tile = tile.reshape(PART, UNIT, TILE)
        slab[narrow, s * PART : (s + 1) * PART] = tile
        held[0][y, s * PART : (s + 1) * PART] = tile
    meta_b[0, 0] = codes
    meta_a[core, x] = codes

    pl.semaphore_wait(barrier, len(peers) + core)

    transfers = block_transfers()
    arrivals, _ = plan(transfers, LEADS[0])
    released = [plan(transfers, lead)[1] for lead in LEADS]
    final = transfers[arrivals[-1][1]][4][1]

    def place(dy, dz):
        return last[dy].at[0] if dz == final else held[dz].at[lax.rem(y + dy, NY)]


    def block_copy(index):
        _, axis, step, there, here, (low, high) = transfers[index]
        device = at(dz=step % NZ) if axis == "z" else at(dy=step % NY)
        window = pl.ds(low, high - low)
        if here[1] == final:
            target = last[here[0]].at[0]
        else:
            target = held[here[1]].at[lax.rem(y + there[0], NY)]
        return remote(
            place(*there).at[window], target.at[window], send_sem.at[index], recv_sem.at[index], device
        )

    def block_arrival(index):
        _, axis, step, _, (dy, dz), (low, high) = transfers[index]
        device = at(dz=step % NZ) if axis == "z" else at(dy=step % NY)
        here = place(dy, dz).at[pl.ds(low, high - low)]
        return remote(here, here, send_sem.at[index], recv_sem.at[index], device)

    sent = []

    def start(copy):
        copy.start()
        sent.append(copy)

    half_started = set()

    def start_after(event):
        first, second = (plan_.get(event, []) for plan_ in released)
        for index in first:
            if index in second:
                start(block_copy(index))
        for which, some, others in ((0, first, second), (1, second, first)):
            for index in some:
                if index in others:
                    continue
                copy = block_copy(index)
                pl.when(core == which)(copy.start)
                if index in half_started:
                    sent.append(copy)
                half_started.add(index)

    start_after(-1)

    def side_copy(index, block, device):
        ref = slab.at[block, pl.ds(0, PACKED)]
        return remote(ref, ref, side_send.at[index], side_recv.at[index], device)

    own_to_sibling = side_copy(0, narrow, sibling)
    for dx in x_peers:
        start(side_copy(dx, narrow, beside(dx, 0)))
    pl.when(core == 1)(own_to_sibling.start)

    for k, d in enumerate(z_peers):
        start(remote(meta_b.at[0, 0], meta_b.at[0, NZ - d], small_send.at[k], small_recv.at[k], at(dz=d)))
    first_x = len(z_peers)
    for k, dx in enumerate(x_peers):
        k += first_x
        own = meta_a.at[core, x]
        start(remote(own, own, small_send.at[k], small_recv.at[k], beside(dx, 0)))
    first_sibling = first_x + len(x_peers)
    first_y = first_sibling + 1
    first_total = first_y + len(y_peers)

    keep_copy = pltpu.make_async_copy(keep, keep_v, local_sem.at[0])
    keep_copy.start()
    blank = jnp.zeros((PART, UNIT, TILE), jnp.bfloat16)
    unit = eye.astype(jnp.bfloat16).reshape(PART, UNIT, TILE)
    for ref, count in [(slab, blocks)] + [(held[dz], NY) for dz in range(NZ) if dz != final] + [(ref, 1) for ref in last]:
        for i in range(count):
            ref[i, PACKED : PACKED + PART] = blank
            ref[i, PACKED + PART : PACKED + 2 * PART] = unit

    def meta_along_y():
        for k, d in enumerate(z_peers):
            here = meta_b.at[0, NZ - d]
            remote(here, here, small_send.at[k], small_recv.at[k], at(dz=d)).wait_recv()
        for k, d in enumerate(y_peers):
            k += first_y
            start(remote(meta_b.at[0], meta_b.at[NY - d], small_send.at[k], small_recv.at[k], at(dy=d)))

    def meta_to_scalars():
        theirs = meta_a.at[1 - core]
        remote(theirs, theirs, small_send.at[first_sibling], small_recv.at[first_sibling], sibling).wait_recv()
        for k, d in enumerate(y_peers):
            k += first_y
            here = meta_b.at[NY - d]
            remote(here, here, small_send.at[k], small_recv.at[k], at(dy=d)).wait_recv()
        for dz in range(NZ):
            for dy in range(NY):
                row = dz * NY + dy
                meta_v[row : row + 1, :] = meta_b[dy, dz, 0:1, :]
        for n in range(blocks):
            row = NZ * NY + n
            meta_v[row : row + 1, :] = meta_a[n % NC, n // NC, 0:1, :]
        copy = pltpu.make_async_copy(meta_v, meta_s, local_sem.at[3])
        copy.start()
        copy.wait()

    def side_arrivals():
        @pl.when(core == 0)
        def _():
            side_copy(0, narrow + 1, sibling).wait_recv()
            own_to_sibling.start()

        for k, dx in enumerate(x_peers):
            source = lax.rem(x + NX - dx, NX) * NC + core
            side_copy(dx, source, beside(dx, 0)).wait_recv()
            start(side_copy(NX - 1 + dx, source, sibling))
            k += first_x
            here = meta_a.at[core, lax.rem(x + NX - dx, NX)]
            remote(here, here, small_send.at[k], small_recv.at[k], beside(dx, 0)).wait_recv()
        ours = meta_a.at[core]
        start(remote(ours, ours, small_send.at[first_sibling], small_recv.at[first_sibling], sibling))
        sent.append(own_to_sibling)

    def tile_of(ref, block, code):
        return ref[block, pl.ds(code * PART, PART)].reshape(TILE, TILE)

    def expand_slab():
        @pl.when(core == 1)
        def _():
            side_copy(0, narrow - 1, sibling).wait_recv()

        for dx in x_peers:
            source = lax.rem(x + NX - dx, NX) * NC + 1 - core
            side_copy(NX - 1 + dx, source, sibling).wait_recv()

        def body(n, carry):
            for r in range(2):
                for c in range(col_tiles):
                    code = meta_s[NZ * NY + n, r * col_tiles + c]
                    dense[n, r * TILE : (r + 1) * TILE, c * TILE : (c + 1) * TILE] = tile_of(slab, n, code)
            return carry

        lax.fori_loop(0, blocks, body, 0)

    row_id = lax.broadcasted_iota(jnp.int32, (2 * TILE, TILE), 0)
    col_id = lax.broadcasted_iota(jnp.int32, (2 * TILE, TILE), 1)

    def strip(ref, row, dy, dz, pair):
        halves = []
        for r in range(2):
            codes = [meta_s[dz * NY + dy, r * col_tiles + pair * 2 + c] for c in range(2)]
            halves.append(jnp.concatenate([tile_of(ref, row, code) for code in codes], axis=1))
        return halves

    def multiply_plane(dz, pair, first):
        halves = []
        for row in range(NY):
            halves += strip(held[dz], row, lax.rem(row - y + NY, NY), dz, pair)
        product = jnp.dot(
            dense[lax.rem(z + dz, NZ)], jnp.concatenate(halves, axis=0), preferred_element_type=jnp.float32
        )
        columns = slice(pair * 2 * TILE, (pair + 1) * 2 * TILE)
        if first:
            out[:, columns] = product
        else:
            out[:, columns] += product

    def multiply_block(dy, pair, finish):
        depth = pl.ds(pl.multiple_of(lax.rem(y + dy, NY) * 2 * TILE, 2 * TILE), 2 * TILE)
        rhs = jnp.concatenate(strip(last[dy], 0, dy, final, pair), axis=0)
        product = jnp.dot(dense[lax.rem(z + final, NZ), :, depth], rhs, preferred_element_type=jnp.float32)
        columns = slice(pair * 2 * TILE, (pair + 1) * 2 * TILE)
        if not finish:
            out[:, columns] += product
            return
        product = out[:, columns] + product
        for half in range(2):
            c = pair * 2 + half
            columns = slice(c * TILE, (c + 1) * TILE)
            value = product[:, half * TILE : (half + 1) * TILE]
            kept = jnp.logical_or(keep_v[:, columns] == 1, row_id + shift == col_id + c * TILE)
            pruned = jnp.where(kept, value * value, 0.0)
            out[:, columns] = pruned
            tot_y[0, c : c + 1, :] = jnp.sum(pruned, axis=0, keepdims=True)

    extras = [(9.0, meta_along_y), (17.0, side_arrivals), (18.0, meta_to_scalars), (21.0, expand_slab)]
    pairs = col_tiles // 2
    left = {}

    def unit_of(index):
        dy, dz = transfers[index][4]
        return (dy, dz) if dz == final else (None, dz)

    for _, index in arrivals:
        left[unit_of(index)] = left.get(unit_of(index), 0) + 1
    blocks_left = NY
    queue, multiplied = [], []
    issued, settled = [], 0
    clock = 0.0

    def run(budget):
        nonlocal clock
        while queue and extras == [] and clock + queue[0][0] <= budget:
            cost, action = queue.pop(0)
            action()
            clock += cost

    for now, index in arrivals:
        end = index == arrivals[-1][1]
        while extras and (end or extras[0][0] <= now):
            extras.pop(0)[1]()
        run(float("inf") if end else now)
        block_arrival(index).wait_recv()
        clock = max(clock, now)
        start_after(index)
        issued.append(len(sent))
        while len(issued) > RETIRE and settled < issued[-RETIRE]:
            sent[settled].wait_send()
            settled += 1
        left[unit_of(index)] -= 1
        if left[unit_of(index)] == 0:
            dy, dz = unit_of(index)
            for pair in range(pairs):
                if dy is None:
                    queue.append((0.3, functools.partial(multiply_plane, dz, pair, not multiplied)))
                else:
                    queue.append((0.1, functools.partial(multiply_block, dy, pair, blocks_left == 1)))
            if dy is None:
                multiplied.append(dz)
            else:
                blocks_left -= 1
    keep_copy.wait()
    if col_tiles < 8:
        tot_y[0] = jnp.ones((8, TILE), jnp.float32)
    run(float("inf"))

    for k, d in enumerate(y_peers):
        k += first_total
        start(remote(tot_y.at[0], tot_y.at[NY - d], small_send.at[k], small_recv.at[k], at(dy=d)))
    before = len(sent) - len(y_peers)
    for copy in sent[settled:before]:
        copy.wait_send()
    for k, d in enumerate(y_peers):
        k += first_total
        here = tot_y.at[NY - d]
        remote(here, here, small_send.at[k], small_recv.at[k], at(dy=d)).wait_recv()
    tot_z[0] = functools.reduce(jnp.add, [tot_y[d] for d in range(NY)])
    first_total_z = first_total + len(y_peers)
    for k, d in enumerate(z_peers):
        k += first_total_z
        start(remote(tot_z.at[0], tot_z.at[NZ - d], small_send.at[k], small_recv.at[k], at(dz=d)))
    for k, d in enumerate(z_peers):
        k += first_total_z
        here = tot_z.at[NZ - d]
        remote(here, here, small_send.at[k], small_recv.at[k], at(dz=d)).wait_recv()
    total = functools.reduce(jnp.add, [tot_z[d] for d in range(NZ)])
    scale = (2 * TILE * NZ * NY) / total
    for c in range(col_tiles):
        columns = slice(c * TILE, (c + 1) * TILE)
        out[:, columns] = out[:, columns] * scale[c : c + 1, :]
    for copy in sent[before:]:
        copy.wait_send()


def shards(values, pattern, keep_mask):
    rows, cols = values.shape
    col_tiles = cols // TILE
    blocks = NX * NC
    transfers = len(block_transfers())
    small = 2 * (NZ - 1) + 2 * (NY - 1) + NX
    return pl.pallas_call(
        functools.partial(kernel, col_tiles),
        out_shape=jax.ShapeDtypeStruct((rows, cols), jnp.float32),
        in_specs=[
            pl.BlockSpec(memory_space=pltpu.HBM),
            pl.BlockSpec(memory_space=pltpu.HBM),
            pl.BlockSpec(memory_space=pltpu.HBM),
        ],
        out_specs=pl.BlockSpec(memory_space=pltpu.VMEM),
        scratch_shapes=[
            [pltpu.VMEM((NY, SLOTS * PART, UNIT, TILE), jnp.bfloat16) for _ in range(NZ)],
            [pltpu.VMEM((1, SLOTS * PART, UNIT, TILE), jnp.bfloat16) for _ in range(NY)],
            pltpu.VMEM((blocks, SLOTS * PART, UNIT, TILE), jnp.bfloat16),
            pltpu.VMEM((blocks, rows, cols), jnp.bfloat16),
            pltpu.VMEM((rows, cols), jnp.int32),
            pltpu.SMEM((2, col_tiles), jnp.int32),
            pltpu.VMEM((rows, cols), jnp.bfloat16),
            pltpu.VMEM((2 * col_tiles, TILE, TILE), jnp.bfloat16),
            pltpu.VMEM((NY, NZ, 8, TILE), jnp.int32),
            pltpu.VMEM((NC, NX, 8, TILE), jnp.int32),
            pltpu.VMEM((NZ * NY + blocks, TILE), jnp.int32),
            pltpu.SMEM((NZ * NY + blocks, TILE), jnp.int32),
            pltpu.VMEM((NY, 8, TILE), jnp.float32),
            pltpu.VMEM((NZ, 8, TILE), jnp.float32),
            pltpu.SemaphoreType.DMA((transfers,)),
            pltpu.SemaphoreType.DMA((transfers,)),
            pltpu.SemaphoreType.DMA((2 * NX - 1,)),
            pltpu.SemaphoreType.DMA((2 * NX - 1,)),
            pltpu.SemaphoreType.DMA((small,)),
            pltpu.SemaphoreType.DMA((small,)),
            pltpu.SemaphoreType.DMA((4,)),
        ],
        compiler_params=pltpu.CompilerParams(
            collective_id=0, has_side_effects=True, vmem_limit_bytes=52 * 1024 * 1024
        ),
        cost_estimate=pl.CostEstimate(flops=2 * rows * cols * 8192, bytes_accessed=12 << 20, transcendentals=0),
    )(*[pltpu.with_memory_space_constraint(operand, pltpu.HBM) for operand in (pattern, values, keep_mask)])


def solution(mesh):
    return jax.shard_map(
        shards,
        mesh=mesh,
        in_specs=(P("wide", "narrow"), P("wide", "narrow"), P("wide", "narrow")),
        out_specs=P("wide", "narrow"),
        check_vma=False,
    )
```
